32 devices in a mesh: groups: 2 (over x), row: 4 (over y, core), dp: 4 (over z).
Axes of the slice: x: 2, y: 2, z: 4, core: 2. Of those that a mesh axis runs over, the one named last changes fastest.
Arguments:
- snapshots: bfloat16 [1024, 4096], P(('groups', 'dp'), 'row'), parts along dimension 0, may hold values from -6 to 6
- enc_weight: bfloat16 [32, 128, 256], P(('row', 'dp')), may hold values from -0.09375 to 0.09375
- hidden_weight: bfloat16 [8192, 256], P('dp'), may hold values from -0.375 to 0.375
- hidden_bias: bfloat16 [8192], P('dp'), may hold values from -3 to 3
- block_weight: bfloat16 [32, 8, 128, 128], P(('row', 'dp')), may hold values from -0.25 to 0.25
- block_ids: int32 [32, 8], P('row'), may hold values from 0 to 63, all different within a row
- block_counts: int32 [32], P('row'), may hold values from 1 to 8, as said below
Outputs:
- enc_grad: float32 [64, 128, 256], P(('groups', 'row', 'dp')), parts along dimension 0
- hidden_weight_grad: float32 [16384, 256], P(('groups', 'dp')), parts along dimension 0
- hidden_bias_grad: float32 [16384], P(('groups', 'dp')), parts along dimension 0
- block_grad: float32 [64, 8, 128, 128], P(('groups', 'row', 'dp')), parts along dimension 0
The draws below stay inside these ranges and needn't reach their ends.
There are 2 independent parts, one for each index of `groups`. The reference program is written for one: setup_inputs(seed, part) draws one part's arguments, and reference() takes and returns one part's arrays. A program takes and returns all parts, laid end to end along the dimension named above; an argument that names none is the same for every part. Nothing has to cross between parts.
Inputs may be any that keep to these rules, and one draw needn't show every extreme that they name: `block_ids`: the 8 block numbers of one tile are distinct. `block_counts`: the live slots of a tile are its first ones; some tile has all 8 live.
All inputs are finite; a program needn't handle non-finite values.
Results may differ from the reference program's by a relative error of at most 0.0043.
Values may be sent and summed in bfloat16 or wider, within the bound.
A program may use at most 128 MiB of HBM per device.

```python
import math
import jax
import jax.numpy as jnp
from jax import lax

L = 256
H = 8192
BLK = 128
KB = 8
NB = 64
TILES = 32
ROWS = 4096
SNAPS = 512


def draw_block_counts(key, part):
    counts = jax.random.randint(key, (TILES,), 1, KB + 1, dtype=jnp.int32)
    return counts.at[0].set(KB)


def level_of(own_key, shape, shards, smallest, high):
    gain, own = 1.0, jax.random.fold_in(own_key, 6)
    for axis_at, shards_of in shards:
        draws = jnp.exp(jax.random.uniform(jax.random.fold_in(own, axis_at), (shards_of,), jnp.float32, smallest / len(shards), high / len(shards)))
        gain = gain * jnp.repeat(draws, shape[axis_at] // shards_of).reshape([-1 if axis == axis_at else 1 for axis in range(len(shape))])
    return gain


def different_ones(stream_key, rows, amount, top, lift):
    sequence = jax.random.permutation(jax.random.fold_in(stream_key, 1), amount)
    pull = sequence
    for power in range(3):
        pull = pull * pull // amount
    pull = pull * lift // amount
    tickets = jax.random.randint(jax.random.fold_in(stream_key, 2), (rows, amount), 0, 4096) + pull
    fixed_rows = jax.random.permutation(jax.random.fold_in(stream_key, 3), rows)[jnp.arange(amount) % rows]
    tickets = jnp.where(jnp.arange(rows)[:, None] == fixed_rows[None, :], 1 << 14, tickets)
    priority = tickets * amount + jnp.arange(amount)
    return lax.top_k(priority.astype(jnp.int32), top)[1].astype(jnp.int32)


def normal_values(key, shape, scale, most, cuts=(), kind=jnp.bfloat16):
    result = jax.random.normal(key, shape, jnp.float32) * scale
    if len(cuts) > 0:
        result = level_of(key, shape, cuts, -0.22, 0.18) * result
    return jnp.clip(result, min=-most, max=most).astype(kind)


def setup_inputs(seed: int = 0, part: int = 0) -> dict:
    splits = jax.random.split(jax.random.key(seed), 8)
    own_keys = jax.random.split(jax.random.fold_in(splits[7], part), 8)
    snapshots = normal_values(own_keys[0], (SNAPS, ROWS), 1.0, 6.0, ((0, 4), (1, 4)))
    enc_weight = normal_values(splits[1], (TILES, BLK, L), ROWS ** -0.5, 0.09375, ((0, 16),))
    hidden_weight = normal_values(splits[2], (H, L), L ** -0.5, 0.375, ((0, 4),))
    hidden_bias = normal_values(splits[3], (H,), 0.7, 3.0, ((0, 4),))
    block_weight = normal_values(splits[4], (TILES, KB, BLK, BLK), (KB * BLK // 2) ** -0.5, 0.25, ((0, 16),))
    block_ids = different_ones(splits[5], TILES, NB, KB, 2048)
    block_counts = draw_block_counts(jax.random.fold_in(splits[7], 71), part)
    return {"snapshots": snapshots, "enc_weight": enc_weight, "hidden_weight": hidden_weight, "hidden_bias": hidden_bias, "block_weight": block_weight, "block_ids": block_ids, "block_counts": block_counts}


def silu_slope(pre):
    sigma = jax.nn.sigmoid(pre)
    return sigma * (1.0 + pre * (1.0 - sigma))

def reference(snapshots, enc_weight, hidden_weight, hidden_bias, block_weight, block_ids, block_counts):
    latent = jnp.dot(snapshots, enc_weight.reshape(ROWS, L), preferred_element_type=jnp.float32)
    latent_b = latent.astype(jnp.bfloat16)
    pre = jnp.dot(latent_b, hidden_weight.T, preferred_element_type=jnp.float32) + hidden_bias.astype(jnp.float32)
    hidden = jax.nn.silu(pre).astype(jnp.bfloat16)
    nblocks = H // BLK
    hidden_blocks = hidden.reshape(SNAPS, nblocks, BLK)
    scale = 1.0 / math.sqrt(SNAPS)
    tile_snaps = snapshots.reshape(SNAPS, TILES, BLK).transpose(1, 0, 2)

    def per_tile(adjoint, inputs):
        snap_tile, weight_tile, ids_tile, count_tile = inputs
        live_slots = (jnp.arange(KB) < count_tile).astype(jnp.float32)
        tile_hidden = (jnp.take(hidden_blocks, ids_tile, axis=1).astype(jnp.float32) * live_slots[None, :, None]).astype(jnp.bfloat16)
        output = jnp.einsum('skc,kcd->sd', tile_hidden.astype(jnp.float32), weight_tile.astype(jnp.float32))
        misfit = ((output - snap_tile.astype(jnp.float32)) * scale).astype(jnp.bfloat16)
        grad_tile = jnp.einsum('skc,sd->kcd', tile_hidden.astype(jnp.float32), misfit.astype(jnp.float32))
        back = jnp.einsum('sd,kcd->skc', misfit.astype(jnp.float32), weight_tile.astype(jnp.float32)) * live_slots[None, :, None]
        onehot = (ids_tile[:, None] == jnp.arange(nblocks)[None, :]).astype(jnp.float32)
        adjoint = adjoint + jnp.einsum('skc,kn->snc', back, onehot, precision=lax.Precision.HIGHEST).reshape(SNAPS, H)
        return (adjoint, grad_tile)
    adjoint, block_grad = lax.scan(per_tile, jnp.zeros((SNAPS, H), jnp.float32), (tile_snaps, block_weight, block_ids, block_counts))
    pre_grad = (adjoint * silu_slope(pre)).astype(jnp.bfloat16)
    hidden_bias_grad = lax.optimization_barrier(jnp.sum(pre_grad.astype(jnp.float32), axis=0))
    hidden_weight_grad = jnp.dot(pre_grad.T, latent_b, preferred_element_type=jnp.float32)
    latent_grad = jnp.dot(pre_grad, hidden_weight, preferred_element_type=jnp.float32).astype(jnp.bfloat16)
    enc_grad = jnp.dot(snapshots.T, latent_grad, preferred_element_type=jnp.float32).reshape(TILES, BLK, L)
    return (enc_grad, hidden_weight_grad, hidden_bias_grad, block_grad)
```

```python
import functools
import math

import jax
import jax.numpy as jnp
from jax import lax
from jax.experimental import pallas as pl
from jax.experimental.pallas import tpu as pltpu
from jax.sharding import PartitionSpec as P

MESH = pl.DeviceIdType.MESH
F32 = jnp.float32
BF16 = jnp.bfloat16
VMEM_LIMIT = 56 * 1024 * 1024


def dot(a, b, ca=1, cb=0):
    return lax.dot_general(a, b, (((ca,), (cb,)), ((), ())), preferred_element_type=F32)


def greet(sizes):
    barrier = pltpu.get_barrier_semaphore()
    total = 0
    for axis, n in sizes.items():
        me = lax.axis_index(axis)
        for i in range(1, n):
            pl.semaphore_signal(
                barrier, inc=1, device_id={axis: lax.rem(me + i, n)}, device_id_type=MESH
            )
        total += n - 1
    pl.semaphore_wait(barrier, total)


class Exchange:
    def __init__(self, axis, n, src_of, dst_of, send, recv):
        self.axis, self.n, self.src_of, self.dst_of = axis, n, src_of, dst_of
        self.send, self.recv = send, recv
        self.me = lax.axis_index(axis)

    def copy(self, peer, slot):
        return pltpu.make_async_remote_copy(
            src_ref=self.src_of(peer),
            dst_ref=self.dst_of(slot),
            send_sem=self.send.at[peer],
            recv_sem=self.recv.at[slot],
            device_id={self.axis: peer},
            device_id_type=MESH,
        )

    def start(self):
        for i in range(1, self.n):
            self.copy(lax.rem(self.me + i, self.n), self.me).start()

    def wait_recv(self):
        for i in range(1, self.n):
            peer = lax.rem(self.me + i, self.n)
            self.copy(peer, peer).wait_recv()

    def wait_send(self):
        for i in range(1, self.n):
            self.copy(lax.rem(self.me + i, self.n), self.me).wait_send()


def forward_kernel(
    row, dp, snap, enc, weight, bias, block,
    hid, pre, lat_all, block_all, wq, snap_all,
    enc_all, bias_all, lat_part, dsend, drecv, rsend, rrecv, lsem,
):
    r, d = lax.axis_index("row"), lax.axis_index("dp")
    cols = snap.shape[1] // dp
    greet({"row": row, "dp": dp})

    def over_dp(k, src_of, dst):
        return Exchange("dp", dp, src_of, lambda s: dst.at[s], dsend.at[k], drecv.at[k])

    def snap_cols(p):
        return snap.at[:, pl.ds(pl.multiple_of(p * cols, cols), cols)]

    x_enc = over_dp(0, lambda p: enc, enc_all)
    x_bias = over_dp(1, lambda p: bias.at[r], bias_all)
    x_w = over_dp(2, lambda p: weight.at[r], wq)
    x_block = over_dp(3, lambda p: block, block_all)
    x_snap = over_dp(4, snap_cols, snap_all)
    x_enc.start()
    x_bias.start()
    x_w.start()
    own_block = pltpu.make_async_copy(block, block_all.at[d], lsem.at[0])
    own_snap = pltpu.make_async_copy(snap_cols(d), snap_all.at[d], lsem.at[1])
    own_block.start()
    own_snap.start()
    enc_all[d] = enc[...]
    bias_all[d] = bias[r]
    wq[d] = weight[r]
    x_enc.wait_recv()
    x_block.start()
    x_snap.start()
    part = jnp.zeros((snap.shape[0], enc.shape[1]), F32)
    for s in range(dp):
        part += dot(snap[:, s * cols : (s + 1) * cols], enc_all[s])
    lat_part[r] = part
    x_lat = Exchange("row", row, lambda p: lat_part.at[r], lambda s: lat_part.at[s], rsend.at[0], rrecv.at[0])
    x_lat.start()
    x_lat.wait_recv()
    total = lat_part[0]
    for s in range(1, row):
        total += lat_part[s]
    latent_b = total.astype(BF16)
    lat_all[d] = latent_b
    x_latb = over_dp(5, lambda p: lat_all.at[d], lat_all)
    x_latb.start()
    x_bias.wait_recv()
    x_w.wait_recv()
    ones = jnp.ones((bias.shape[1], snap.shape[0]), BF16)
    for s in range(dp):
        v = dot(wq[s], latent_b, 1, 1) + dot(bias_all[s], ones, 0, 0)
        pre[s] = v
        hid[s, r] = jax.nn.silu(v).astype(BF16)
    x_hid = Exchange("row", row, lambda p: hid.at[:, r], lambda s: hid.at[:, s], rsend.at[1], rrecv.at[1])
    x_hid.start()
    own_block.wait()
    own_snap.wait()
    for x in (x_hid, x_latb, x_block, x_snap):
        x.wait_recv()
    for x in (x_enc, x_bias, x_w, x_block, x_snap, x_lat, x_latb, x_hid):
        x.wait_send()


def decode_kernel(scale, ids, counts, hid, block, snap, slots_ref, mis_ref, adj_ref, adj):
    tiles, slots, blk, _ = block.shape
    adj[...] = jnp.zeros_like(adj)

    def tile(t, _):
        count = counts[t]
        out = jnp.zeros((snap.shape[0], blk), F32)
        for k in range(slots):
            live = (k < count).astype(F32)
            h = (hid[ids[t, k]].astype(F32) * live).astype(BF16)
            slots_ref[t, k] = h
            out += dot(h, block[t, k], 0, 0)
        here = snap[:, pl.ds(pl.multiple_of(t * blk, blk), blk)].astype(F32)
        misfit = ((out - here) * scale).astype(BF16)
        mis_ref[t] = misfit
        for k in range(slots):
            live = (k < count).astype(F32)
            adj[ids[t, k]] += dot(block[t, k], misfit, 1, 1) * live
        return 0

    lax.fori_loop(0, tiles, tile, 0)
    adj_ref[...] = adj[...].astype(BF16)


def backward_kernel(
    row, dp, adj, slots, mis, pre, lat_all, wq, snap_all,
    wgrad, bgrad, enc_grad, block_grad,
    adj_all, slots_all, mis_all, pg, pg_all, lg_part, lg_all,
    dsend, drecv, rsend, rrecv,
):
    r, d = lax.axis_index("row"), lax.axis_index("dp")
    greet({"row": row, "dp": dp})

    def over_dp(k, src_of, dst):
        return Exchange("dp", dp, src_of, lambda s: dst.at[s], dsend.at[k], drecv.at[k])

    def over_row(k, src_of, dst):
        return Exchange("row", row, src_of, lambda s: dst.at[s], rsend.at[k], rrecv.at[k])

    x_adj = over_row(0, lambda p: adj.at[:, p], adj_all)
    x_adj.start()
    x_mis = over_dp(0, lambda p: mis.at[p], mis_all)
    x_slots = over_dp(1, lambda p: slots.at[p], slots_all)
    x_mis.start()
    x_slots.start()
    adj_all[r] = adj[:, r]
    mis_all[d] = mis[d]
    slots_all[d] = slots[d]
    x_adj.wait_recv()
    part = jnp.zeros((mis.shape[2], lat_all.shape[2]), F32)
    for s in range(dp):
        a = adj_all[0, s].astype(F32)
        for q in range(1, row):
            a += adj_all[q, s].astype(F32)
        v = pre[s]
        sigma = jax.nn.sigmoid(v)
        g = (a * (sigma * (1.0 + v * (1.0 - sigma)))).astype(BF16)
        pg[s] = g
        part += dot(g, wq[s], 0, 0)
    pg_all[d] = pg[d]
    lg_part[r] = part
    x_lg = over_row(1, lambda p: lg_part.at[r], lg_part)
    x_pg = over_dp(2, lambda p: pg.at[p], pg_all)
    x_lg.start()
    x_pg.start()
    x_lg.wait_recv()
    total = lg_part[0]
    for s in range(1, row):
        total += lg_part[s]
    lg_all[d] = total.astype(BF16)
    x_lgb = over_dp(3, lambda p: lg_all.at[d], lg_all)
    x_lgb.start()
    x_pg.wait_recv()
    w = jnp.zeros(wgrad.shape[1:], F32)
    b = jnp.zeros(bgrad.shape[1:], F32)
    ones = jnp.ones((bgrad.shape[1], mis.shape[2]), BF16)
    for s in range(dp):
        w += dot(pg_all[s], lat_all[s])
        b += dot(ones, pg_all[s], 1, 1)
    wgrad[r] = w
    bgrad[r] = b
    x_w = over_row(2, lambda p: wgrad.at[r], wgrad)
    x_b = over_row(3, lambda p: bgrad.at[r], bgrad)
    x_w.start()
    x_b.start()
    x_mis.wait_recv()
    x_slots.wait_recv()

    def slot(k, _):
        for t in range(block_grad.shape[0]):
            o = dot(slots_all[0, t, k], mis_all[0, t])
            for s in range(1, dp):
                o += dot(slots_all[s, t, k], mis_all[s, t])
            block_grad[t, k] = o
        return 0

    lax.fori_loop(0, block_grad.shape[1], slot, 0)
    x_lgb.wait_recv()
    e = dot(snap_all[0], lg_all[0], 0, 0)
    for s in range(1, dp):
        e += dot(snap_all[s], lg_all[s], 0, 0)
    enc_grad[...] = e
    x_w.wait_recv()
    x_b.wait_recv()
    for x in (x_adj, x_mis, x_slots, x_lg, x_pg, x_lgb, x_w, x_b):
        x.wait_send()


def on_device(
    row, dp, snapshots, enc_weight, hidden_weight, hidden_bias, block_weight, block_ids, block_counts
):
    batch = snapshots.shape[0]
    own, slots, blk = block_weight.shape[:3]
    latent = enc_weight.shape[2]
    shard = hidden_weight.shape[0]
    part = shard // row
    tiles = own * dp
    cols = own * blk
    vmem = pl.BlockSpec(memory_space=pltpu.VMEM)
    smem = pl.BlockSpec(memory_space=pltpu.SMEM)
    dma = pltpu.SemaphoreType.DMA
    sds = jax.ShapeDtypeStruct
    bias = jnp.pad(hidden_bias.reshape(row, 1, part), ((0, 0), (0, 15), (0, 0)))
    hid, pre, lat_all, block_all, wq, snap_all = pl.pallas_call(
        functools.partial(forward_kernel, row, dp),
        out_shape=(
            sds((dp, row, part, batch), BF16),
            sds((dp, part, batch), F32),
            sds((dp, batch, latent), BF16),
            sds((dp, own, slots, blk, blk), BF16),
            sds((dp, part, latent), BF16),
            sds((dp, batch, cols), BF16),
        ),
        in_specs=[vmem] * 5,
        out_specs=[vmem] * 6,
        scratch_shapes=[
            pltpu.VMEM((dp, cols, latent), BF16),
            pltpu.VMEM((dp, 16, part), BF16),
            pltpu.VMEM((row, batch, latent), F32),
            dma((6, dp)), dma((6, dp)), dma((2, row)), dma((2, row)), dma((2,)),
        ],
        compiler_params=pltpu.CompilerParams(
            collective_id=0, has_side_effects=True, vmem_limit_bytes=VMEM_LIMIT
        ),
        name="forward",
    )(
        snapshots,
        enc_weight.reshape(cols, latent),
        hidden_weight.reshape(row, part, latent),
        bias,
        block_weight,
    )
    nblocks = dp * shard // blk
    scale = 1.0 / math.sqrt(batch * dp)
    tile_slots, misfit, adj = pl.pallas_call(
        functools.partial(decode_kernel, scale),
        out_shape=(
            sds((tiles, slots, blk, batch), BF16),
            sds((tiles, batch, blk), BF16),
            sds((nblocks, blk, batch), BF16),
        ),
        in_specs=[smem, smem, vmem, vmem, vmem],
        out_specs=[vmem] * 3,
        scratch_shapes=[pltpu.VMEM((nblocks, blk, batch), F32)],
        compiler_params=pltpu.CompilerParams(vmem_limit_bytes=VMEM_LIMIT),
        name="decode",
    )(
        block_ids,
        block_counts,
        hid.reshape(nblocks, blk, batch),
        block_all.reshape(tiles, slots, blk, blk),
        snapshots,
    )
    weight_grad, bias_grad, enc_grad, block_grad = pl.pallas_call(
        functools.partial(backward_kernel, row, dp),
        out_shape=(
            sds((row, part, latent), F32),
            sds((row, 8, part), F32),
            sds((cols, latent), F32),
            sds((own, slots, blk, blk), F32),
        ),
        in_specs=[vmem] * 7,
        out_specs=[vmem] * 4,
        scratch_shapes=[
            pltpu.VMEM((row, dp, part, batch), BF16),
            pltpu.VMEM((dp, own, slots, blk, batch), BF16),
            pltpu.VMEM((dp, own, batch, blk), BF16),
            pltpu.VMEM((dp, part, batch), BF16),
            pltpu.VMEM((dp, part, batch), BF16),
            pltpu.VMEM((row, batch, latent), F32),
            pltpu.VMEM((dp, batch, latent), BF16),
            dma((4, dp)), dma((4, dp)), dma((4, row)), dma((4, row)),
        ],
        compiler_params=pltpu.CompilerParams(
            collective_id=1, has_side_effects=True, vmem_limit_bytes=VMEM_LIMIT
        ),
        name="backward",
    )(
        adj.reshape(dp, row, part, batch),
        tile_slots.reshape(dp, own, slots, blk, batch),
        misfit.reshape(dp, own, batch, blk),
        pre,
        lat_all,
        wq,
        snap_all,
    )
    return (
        enc_grad.reshape(own, blk, latent),
        weight_grad.reshape(shard, latent),
        bias_grad[:, 0, :].reshape(shard),
        block_grad,
    )


def solution(mesh):
    in_specs = (
        P(("groups", "dp"), "row"),
        P(("row", "dp"), None, None),
        P("dp", None),
        P("dp"),
        P(("row", "dp"), None, None, None),
        P("row", None),
        P("row"),
    )
    out_specs = (
        P(("groups", "row", "dp"), None, None),
        P(("groups", "dp"), None),
        P(("groups", "dp")),
        P(("groups", "row", "dp"), None, None, None),
    )
    return jax.shard_map(
        functools.partial(on_device, mesh.shape["row"], mesh.shape["dp"]),
        mesh=mesh, in_specs=in_specs, out_specs=out_specs, check_vma=False,
    )
```

```python
import functools
import math

import jax
import jax.numpy as jnp
from jax import lax
from jax.experimental import pallas as pl
from jax.experimental.pallas import tpu as pltpu
from jax.sharding import PartitionSpec as P

MESH = pl.DeviceIdType.MESH
F32 = jnp.float32
BF16 = jnp.bfloat16
VMEM_LIMIT = 56 * 1024 * 1024


def dot(a, b, ca=1, cb=0):
    return lax.dot_general(a, b, (((ca,), (cb,)), ((), ())), preferred_element_type=F32)


def greet(sizes):
    barrier = pltpu.get_barrier_semaphore()
    total = 0
    for axis, n in sizes.items():
        me = lax.axis_index(axis)
        for i in range(1, n):
            pl.semaphore_signal(
                barrier, inc=1, device_id={axis: lax.rem(me + i, n)}, device_id_type=MESH
            )
        total += n - 1
    pl.semaphore_wait(barrier, total)


class Exchange:
    def __init__(self, axis, n, src_of, dst_of, send, recv):
        self.axis, self.n, self.src_of, self.dst_of = axis, n, src_of, dst_of
        self.send, self.recv = send, recv
        self.me = lax.axis_index(axis)

    def copy(self, peer, slot):
        return pltpu.make_async_remote_copy(
            src_ref=self.src_of(peer),
            dst_ref=self.dst_of(slot),
            send_sem=self.send.at[peer],
            recv_sem=self.recv.at[slot],
            device_id={self.axis: peer},
            device_id_type=MESH,
        )

    def start(self):
        for i in range(1, self.n):
            self.copy(lax.rem(self.me + i, self.n), self.me).start()

    def wait_recv(self):
        for i in range(1, self.n):
            peer = lax.rem(self.me + i, self.n)
            self.copy(peer, peer).wait_recv()

    def wait_send(self):
        for i in range(1, self.n):
            self.copy(lax.rem(self.me + i, self.n), self.me).wait_send()


class Chain:
    def __init__(self, axis, n, dst_of, send, recv):
        self.axis, self.n, self.dst_of = axis, n, dst_of
        self.send, self.recv = send, recv
        self.me = lax.axis_index(axis)

    def copy(self, slot, way, sem):
        return pltpu.make_async_remote_copy(
            src_ref=self.dst_of(slot),
            dst_ref=self.dst_of(slot),
            send_sem=self.send.at[sem],
            recv_sem=self.recv.at[slot],
            device_id={self.axis: self.me + way},
            device_id_type=MESH,
        )

    def each(self, step, act):
        me, n = self.me, self.n
        for way in (1, -1):
            slot = me - way * step
            sem = slot if step or way == 1 else n
            there, held = me + way, slot
            ok = (there >= 0) & (there < n) & (held >= 0) & (held < n)

            @pl.when(ok)
            def _():
                act(self.copy(slot, way, sem))

    def arrived(self, step):
        for way in (1, -1):
            slot = self.me - way * step

            @pl.when((slot >= 0) & (slot < self.n))
            def _():
                self.copy(slot, -way, slot).wait_recv()

    def start(self):
        self.each(0, lambda c: c.start())

    def forward(self, step):
        self.arrived(step)
        self.each(step, lambda c: c.start())

    def wait_send(self):
        for step in range(self.n - 1):
            self.each(step, lambda c: c.wait_send())


class RowRelay:
    def __init__(self, row, dst_of, send, recv):
        self.row, self.dst_of, self.send, self.recv = row, dst_of, send, recv
        self.me = lax.axis_index("row")
        self.sib = self.me + 1 - 2 * lax.rem(self.me, 2)
        self.peers = [lax.rem(self.me + 2 * i, row) for i in range(1, row // 2)]

    def copy(self, slot, to, sem):
        return pltpu.make_async_remote_copy(
            src_ref=self.dst_of(slot),
            dst_ref=self.dst_of(slot),
            send_sem=self.send.at[sem],
            recv_sem=self.recv.at[slot],
            device_id={"row": to},
            device_id_type=MESH,
        )

    def start(self):
        for p in self.peers:
            self.copy(self.me, p, p).start()
        self.copy(self.me, self.sib, self.sib).start()

    def forward(self):
        for p in self.peers:
            self.copy(p, p, p).wait_recv()
            self.copy(p, self.sib, self.row + p).start()

    def wait_recv(self):
        for p in [self.me, *self.peers]:
            slot = p + 1 - 2 * lax.rem(p, 2)
            self.copy(slot, self.sib, slot).wait_recv()

    def wait_send(self):
        for p in self.peers:
            self.copy(self.me, p, p).wait_send()
            self.copy(p, self.sib, self.row + p).wait_send()
        self.copy(self.me, self.sib, self.sib).wait_send()


def forward_kernel(
    row, dp, snap, enc, weight, bias, block,
    hid, pre, lat_all, block_all, w_all, snap_all, bias_all,
    enc_all, lat_part, dsend, drecv, csend, crecv, rsend, rrecv, wsend, wrecv, lsem,
):
    r, d = lax.axis_index("row"), lax.axis_index("dp")
    cols = snap.shape[1] // dp
    batch = snap.shape[0]
    greet({"row": row, "dp": dp})

    def over_dp(k, src_of, dst):
        return Exchange("dp", dp, src_of, lambda s: dst.at[s], dsend.at[k], drecv.at[k])

    def snap_cols(p):
        return snap.at[:, pl.ds(pl.multiple_of(p * cols, cols), cols)]

    def w_slot(s):
        return RowRelay(row, lambda q: w_all.at[s, q], wsend.at[s], wrecv.at[s])

    def w_arrived(step):
        x_w.forward(step)
        for way in (1, -1):
            s = d - way * step

            @pl.when((s >= 0) & (s < dp))
            def _():
                w_slot(s).start()

    x_enc = Chain("dp", dp, lambda s: enc_all.at[s], csend.at[0], crecv.at[0])
    x_w = Chain("dp", dp, lambda s: w_all.at[s, r], csend.at[1], crecv.at[1])
    x_block = Chain("dp", dp, lambda s: block_all.at[s], csend.at[2], crecv.at[2])
    x_bias = over_dp(0, lambda p: bias, bias_all)
    x_snap = over_dp(1, snap_cols, snap_all)
    own_block = pltpu.make_async_copy(block, block_all.at[d], lsem.at[0])
    own_snap = pltpu.make_async_copy(snap_cols(d), snap_all.at[d], lsem.at[1])
    own_block.start()
    own_snap.start()
    enc_all[d] = enc[...]
    x_enc.start()
    w_all[d, r] = weight[r]
    x_w.start()
    w_slot(d).start()
    bias_all[d] = bias[...]
    x_bias.start()
    for step in range(1, dp - 1):
        x_enc.forward(step)
        w_arrived(step)
    own_block.wait()
    x_block.start()
    x_snap.start()
    x_enc.forward(dp - 1)
    part = jnp.zeros((batch, enc.shape[1]), F32)
    for s in range(dp):
        part += dot(snap[:, s * cols : (s + 1) * cols], enc_all[s])
    lat_part[r] = part
    x_lat = Exchange("row", row, lambda p: lat_part.at[r], lambda s: lat_part.at[s], rsend, rrecv)
    x_lat.start()
    w_arrived(dp - 1)
    x_lat.wait_recv()
    total = lat_part[0]
    for s in range(1, row):
        total += lat_part[s]
    latent_b = total.astype(BF16)
    lat_all[d] = latent_b
    x_latb = over_dp(2, lambda p: lat_all.at[d], lat_all)
    x_latb.start()
    if dp > 2:
        x_block.forward(1)
    x_bias.wait_recv()
    lines = lax.broadcasted_iota(jnp.int32, (bias.shape[0], batch), 0)

    def pre_of(s, q):
        pick = jnp.where(lines == q, 1.0, 0.0).astype(BF16)
        return dot(w_all[s, q], lat_all[d], 1, 1) + dot(bias_all[s], pick, 0, 0)

    for s in range(dp):
        pre[s] = pre_of(s, r)
    for s in range(dp):
        w_slot(s).forward()
    for step in range(2, dp - 1):
        x_block.forward(step)

    def hid_of(s, _):
        w_slot(s).wait_recv()
        for q in range(row):
            hid[s, q] = jax.nn.silu(pre_of(s, q)).astype(BF16)
        return 0

    lax.fori_loop(0, dp, hid_of, 0)
    own_snap.wait()
    x_block.arrived(dp - 1)
    for x in (x_latb, x_snap):
        x.wait_recv()
    for x in (x_enc, x_bias, x_w, x_block, x_snap, x_lat, x_latb):
        x.wait_send()
    for s in range(dp):
        w_slot(s).wait_send()


def decode_kernel(scale, ids, counts, hid, block, snap, mis_ref, adj_ref, adj):
    tiles, slots, blk, _ = block.shape
    adj[...] = jnp.zeros_like(adj)

    def tile(t, _):
        count = counts[t]
        out = jnp.zeros((snap.shape[0], blk), F32)
        for k in range(slots):
            live = (k < count).astype(F32)
            out += dot(hid[ids[t, k]], block[t, k], 0, 0) * live
        here = snap[:, pl.ds(pl.multiple_of(t * blk, blk), blk)].astype(F32)
        misfit = ((out - here) * scale).astype(BF16)
        mis_ref[t] = misfit
        for k in range(slots):
            live = (k < count).astype(F32)
            adj[ids[t, k]] += dot(block[t, k], misfit, 1, 1) * live
        return 0

    lax.fori_loop(0, tiles, tile, 0)
    adj_ref[...] = adj[...].astype(BF16)


def block_grad_kernel(ids, counts, w, bias, lat, mis, grad):
    own, slots, blk, _ = grad.shape
    dp = mis.shape[0]
    ones = jnp.ones((bias.shape[1], mis.shape[2]), BF16)

    def slot(k, _):
        for t in range(own):
            j = ids[t, k]
            live = (k < counts[t]).astype(F32)
            shift = dot(bias[j], ones, 0, 0)
            o = jnp.zeros((blk, blk), F32)
            for s in range(dp):
                h = jax.nn.silu(dot(w[j], lat[s], 1, 1) + shift).astype(BF16)
                o += dot(h, mis[s, t])
            grad[t, k] = o * live
        return 0

    lax.fori_loop(0, slots, slot, 0)


def backward_kernel(
    row, dp, adj, mis, pre, lat_all, w_all, snap_all,
    wgrad, bgrad, enc_grad, mis_all,
    adj_all, pg, pg_all, lg_part, lg_all,
    dsend, drecv, rsend, rrecv, wsend, wrecv,
):
    r, d = lax.axis_index("row"), lax.axis_index("dp")
    greet({"row": row, "dp": dp})

    def over_dp(k, src_of, dst):
        return Exchange("dp", dp, src_of, lambda s: dst.at[s], dsend.at[k], drecv.at[k])

    def over_row(k, src_of, dst):
        return Exchange("row", row, src_of, lambda s: dst.at[s], rsend.at[k], rrecv.at[k])

    x_adj = over_row(0, lambda p: adj.at[:, p], adj_all)
    x_adj.start()
    x_mis = over_dp(0, lambda p: mis.at[p], mis_all)
    x_mis.start()
    adj_all[r] = adj[:, r]
    mis_all[d] = mis[d]
    x_adj.wait_recv()
    part = jnp.zeros((mis.shape[2], lat_all.shape[2]), F32)
    for s in range(dp):
        a = adj_all[0, s].astype(F32)
        for q in range(1, row):
            a += adj_all[q, s].astype(F32)
        v = pre[s]
        sigma = jax.nn.sigmoid(v)
        g = (a * (sigma * (1.0 + v * (1.0 - sigma)))).astype(BF16)
        pg[s] = g
    x_pg = over_dp(1, lambda p: pg.at[p], pg_all)
    x_pg.start()
    for s in range(dp):
        part += dot(pg[s], w_all[s, r], 0, 0)
    pg_all[d] = pg[d]
    lg_part[r] = part
    x_lg = over_row(1, lambda p: lg_part.at[r], lg_part)
    x_lg.start()
    x_lg.wait_recv()
    total = lg_part[0]
    for s in range(1, row):
        total += lg_part[s]
    lg_all[d] = total.astype(BF16)
    x_lgb = over_dp(2, lambda p: lg_all.at[d], lg_all)
    x_lgb.start()
    x_pg.wait_recv()
    w = jnp.zeros(wgrad.shape[1:], F32)
    b = jnp.zeros(bgrad.shape[1:], F32)
    ones = jnp.ones((bgrad.shape[1], mis.shape[2]), BF16)
    for s in range(dp):
        w += dot(pg_all[s], lat_all[s])
    wgrad[r] = w
    x_w = RowRelay(row, lambda q: wgrad.at[q], wsend, wrecv)
    x_w.start()
    for s in range(dp):
        b += dot(ones, pg_all[s], 1, 1)
    bgrad[r] = b
    x_b = over_row(2, lambda p: bgrad.at[r], bgrad)
    x_b.start()
    x_lgb.wait_recv()
    e = dot(snap_all[0], lg_all[0], 0, 0)
    for s in range(1, dp):
        e += dot(snap_all[s], lg_all[s], 0, 0)
    enc_grad[...] = e
    x_w.forward()
    x_mis.wait_recv()
    x_b.wait_recv()
    x_w.wait_recv()
    for x in (x_adj, x_mis, x_lg, x_pg, x_lgb, x_w, x_b):
        x.wait_send()


def on_device(
    row, dp, snapshots, enc_weight, hidden_weight, hidden_bias, block_weight, block_ids, block_counts
):
    batch = snapshots.shape[0]
    own, slots, blk = block_weight.shape[:3]
    latent = enc_weight.shape[2]
    shard = hidden_weight.shape[0]
    part = shard // row
    tiles = own * dp
    cols = own * blk
    vmem = pl.BlockSpec(memory_space=pltpu.VMEM)
    smem = pl.BlockSpec(memory_space=pltpu.SMEM)
    dma = pltpu.SemaphoreType.DMA
    sds = jax.ShapeDtypeStruct
    bias = jnp.pad(hidden_bias.reshape(row, part), ((0, -row % 16), (0, 0)))
    hid, pre, lat_all, block_all, w_all, snap_all, bias_all = pl.pallas_call(
        functools.partial(forward_kernel, row, dp),
        out_shape=(
            sds((dp, row, part, batch), BF16),
            sds((dp, part, batch), F32),
            sds((dp, batch, latent), BF16),
            sds((dp, own, slots, blk, blk), BF16),
            sds((dp, row, part, latent), BF16),
            sds((dp, batch, cols), BF16),
            sds((dp, *bias.shape), BF16),
        ),
        in_specs=[vmem] * 5,
        out_specs=[vmem] * 7,
        scratch_shapes=[
            pltpu.VMEM((dp, cols, latent), BF16),
            pltpu.VMEM((row, batch, latent), F32),
            dma((3, dp)), dma((3, dp)), dma((3, dp + 1)), dma((3, dp)), dma((row,)), dma((row,)),
            dma((dp, 2 * row)), dma((dp, row)), dma((2,)),
        ],
        compiler_params=pltpu.CompilerParams(
            collective_id=0, has_side_effects=True, vmem_limit_bytes=VMEM_LIMIT
        ),
        name="forward",
    )(
        snapshots,
        enc_weight.reshape(cols, latent),
        hidden_weight.reshape(row, part, latent),
        bias,
        block_weight,
    )
    nblocks = dp * shard // blk
    scale = 1.0 / math.sqrt(batch * dp)
    misfit, adj = pl.pallas_call(
        functools.partial(decode_kernel, scale),
        out_shape=(
            sds((tiles, batch, blk), BF16),
            sds((nblocks, blk, batch), BF16),
        ),
        in_specs=[smem, smem, vmem, vmem, vmem],
        out_specs=[vmem] * 2,
        scratch_shapes=[pltpu.VMEM((nblocks, blk, batch), F32)],
        compiler_params=pltpu.CompilerParams(vmem_limit_bytes=VMEM_LIMIT),
        name="decode",
    )(
        block_ids,
        block_counts,
        hid.reshape(nblocks, blk, batch),
        block_all.reshape(tiles, slots, blk, blk),
        snapshots,
    )
    weight_grad, bias_grad, enc_grad, mis_all = pl.pallas_call(
        functools.partial(backward_kernel, row, dp),
        out_shape=(
            sds((row, part, latent), F32),
            sds((row, 8, part), F32),
            sds((cols, latent), F32),
            sds((dp, own, batch, blk), BF16),
        ),
        in_specs=[vmem] * 6,
        out_specs=[vmem] * 4,
        scratch_shapes=[
            pltpu.VMEM((row, dp, part, batch), BF16),
            pltpu.VMEM((dp, part, batch), BF16),
            pltpu.VMEM((dp, part, batch), BF16),
            pltpu.VMEM((row, batch, latent), F32),
            pltpu.VMEM((dp, batch, latent), BF16),
            dma((3, dp)), dma((3, dp)), dma((3, row)), dma((3, row)), dma((2 * row,)), dma((row,)),
        ],
        compiler_params=pltpu.CompilerParams(
            collective_id=1, has_side_effects=True, vmem_limit_bytes=VMEM_LIMIT
        ),
        name="backward",
    )(
        adj.reshape(dp, row, part, batch),
        misfit.reshape(dp, own, batch, blk),
        pre,
        lat_all,
        w_all,
        snap_all,
    )
    first = lax.axis_index("dp") * own
    bias_lines = bias_all[:, :row].reshape(nblocks, 1, blk)
    block_grad = pl.pallas_call(
        block_grad_kernel,
        out_shape=sds((own, slots, blk, blk), F32),
        in_specs=[smem, smem, vmem, vmem, vmem, vmem],
        out_specs=vmem,
        compiler_params=pltpu.CompilerParams(vmem_limit_bytes=VMEM_LIMIT),
        name="block_grad",
    )(
        lax.dynamic_slice_in_dim(block_ids, first, own),
        lax.dynamic_slice_in_dim(block_counts, first, own),
        w_all.reshape(nblocks, blk, latent),
        jnp.pad(bias_lines, ((0, 0), (0, 15), (0, 0))),
        lat_all,
        mis_all,
    )
    return (
        enc_grad.reshape(own, blk, latent),
        weight_grad.reshape(shard, latent),
        bias_grad[:, 0, :].reshape(shard),
        block_grad,
    )


def solution(mesh):
    in_specs = (
        P(("groups", "dp"), "row"),
        P(("row", "dp"), None, None),
        P("dp", None),
        P("dp"),
        P(("row", "dp"), None, None, None),
        P("row", None),
        P("row"),
    )
    out_specs = (
        P(("groups", "row", "dp"), None, None),
        P(("groups", "dp"), None),
        P(("groups", "dp")),
        P(("groups", "row", "dp"), None, None, None),
    )
    return jax.shard_map(
        functools.partial(on_device, mesh.shape["row"], mesh.shape["dp"]),
        mesh=mesh, in_specs=in_specs, out_specs=out_specs, check_vma=False,
    )
```

```python
import functools
import math

import jax
import jax.numpy as jnp
from jax import lax
from jax.experimental import pallas as pl
from jax.experimental.pallas import tpu as pltpu
from jax.sharding import PartitionSpec as P

MESH = pl.DeviceIdType.MESH
F32 = jnp.float32
BF16 = jnp.bfloat16
VMEM_LIMIT = 56 * 1024 * 1024


def dot(a, b, ca=1, cb=0):
    return lax.dot_general(a, b, (((ca,), (cb,)), ((), ())), preferred_element_type=F32)


def greet(sizes):
    barrier = pltpu.get_barrier_semaphore()
    total = 0
    for axis, n in sizes.items():
        me = lax.axis_index(axis)
        for i in range(1, n):
            pl.semaphore_signal(
                barrier, inc=1, device_id={axis: lax.rem(me + i, n)}, device_id_type=MESH
            )
        total += n - 1
    pl.semaphore_wait(barrier, total)


class Exchange:
    def __init__(self, axis, n, src_of, dst_of, send, recv):
        self.axis, self.n, self.src_of, self.dst_of = axis, n, src_of, dst_of
        self.send, self.recv = send, recv
        self.me = lax.axis_index(axis)

    def copy(self, peer, slot):
        return pltpu.make_async_remote_copy(
            src_ref=self.src_of(peer),
            dst_ref=self.dst_of(slot),
            send_sem=self.send.at[peer],
            recv_sem=self.recv.at[slot],
            device_id={self.axis: peer},
            device_id_type=MESH,
        )

    def start(self):
        for i in range(1, self.n):
            self.copy(lax.rem(self.me + i, self.n), self.me).start()

    def wait_recv(self):
        for i in range(1, self.n):
            peer = lax.rem(self.me + i, self.n)
            self.copy(peer, peer).wait_recv()

    def wait_send(self):
        for i in range(1, self.n):
            self.copy(lax.rem(self.me + i, self.n), self.me).wait_send()


class Chain:
    def __init__(self, axis, n, dst_of, send, recv):
        self.axis, self.n, self.dst_of = axis, n, dst_of
        self.send, self.recv = send, recv
        self.me = lax.axis_index(axis)

    def copy(self, slot, way, sem):
        return pltpu.make_async_remote_copy(
            src_ref=self.dst_of(slot),
            dst_ref=self.dst_of(slot),
            send_sem=self.send.at[sem],
            recv_sem=self.recv.at[slot],
            device_id={self.axis: self.me + way},
            device_id_type=MESH,
        )

    def each(self, step, act):
        me, n = self.me, self.n
        for way in (1, -1):
            slot = me - way * step
            sem = slot if step or way == 1 else n
            there, held = me + way, slot
            ok = (there >= 0) & (there < n) & (held >= 0) & (held < n)

            @pl.when(ok)
            def _():
                act(self.copy(slot, way, sem))

    def arrived(self, step):
        for way in (1, -1):
            slot = self.me - way * step

            @pl.when((slot >= 0) & (slot < self.n))
            def _():
                self.copy(slot, -way, slot).wait_recv()

    def start(self):
        self.each(0, lambda c: c.start())

    def forward(self, step):
        self.arrived(step)
        self.each(step, lambda c: c.start())

    def wait_send(self):
        for step in range(self.n - 1):
            self.each(step, lambda c: c.wait_send())


class Spread:
    def __init__(self, ng, part_of, send, recv):
        self.ng, self.part_of, self.send, self.recv = ng, part_of, send, recv
        self.me = lax.axis_index("groups")
        self.peers = [lax.rem(self.me + i, ng) for i in range(1, ng)]

    def copy(self, slot, part, peer):
        return pltpu.make_async_remote_copy(
            src_ref=self.part_of(slot, part),
            dst_ref=self.part_of(slot, part),
            send_sem=self.send.at[slot * self.ng + peer],
            recv_sem=self.recv.at[slot * self.ng + part],
            device_id={"groups": peer},
            device_id_type=MESH,
        )

    def start(self, slot):
        for p in self.peers:
            self.copy(slot, self.me, p).start()

    def wait_recv(self, slot):
        for p in self.peers:
            self.copy(slot, p, p).wait_recv()

    def wait_send(self, slot):
        for p in self.peers:
            self.copy(slot, self.me, p).wait_send()


class RowRelay:
    def __init__(self, row, dst_of, send, recv):
        self.row, self.dst_of, self.send, self.recv = row, dst_of, send, recv
        self.me = lax.axis_index("row")
        self.sib = self.me + 1 - 2 * lax.rem(self.me, 2)
        self.peers = [lax.rem(self.me + 2 * i, row) for i in range(1, row // 2)]

    def copy(self, slot, to, sem):
        return pltpu.make_async_remote_copy(
            src_ref=self.dst_of(slot),
            dst_ref=self.dst_of(slot),
            send_sem=self.send.at[sem],
            recv_sem=self.recv.at[slot],
            device_id={"row": to},
            device_id_type=MESH,
        )

    def start(self):
        for p in self.peers:
            self.copy(self.me, p, p).start()
        self.copy(self.me, self.sib, self.sib).start()

    def forward(self):
        for p in self.peers:
            self.copy(p, p, p).wait_recv()
            self.copy(p, self.sib, self.row + p).start()

    def wait_recv(self):
        for p in [self.me, *self.peers]:
            slot = p + 1 - 2 * lax.rem(p, 2)
            self.copy(slot, self.sib, slot).wait_recv()

    def wait_send(self):
        for p in self.peers:
            self.copy(self.me, p, p).wait_send()
            self.copy(p, self.sib, self.row + p).wait_send()
        self.copy(self.me, self.sib, self.sib).wait_send()


def forward_kernel(
    ng, row, dp, snap, enc, weight, bias, block,
    hid, pre, lat_all, block_all, w_all, snap_all, bias_all,
    enc_all, lat_part, dsend, drecv, csend, crecv, rsend, rrecv, wsend, wrecv, gsend, grecv, lsem,
):
    r, d = lax.axis_index("row"), lax.axis_index("dp")
    cols = snap.shape[1] // dp
    batch = snap.shape[0]
    g = lax.axis_index("groups")
    others = [lax.rem(d + i, dp) for i in range(1, dp)]
    greet({"groups": ng, "row": row, "dp": dp})

    def over_dp(k, src_of, dst):
        return Exchange("dp", dp, src_of, lambda s: dst.at[s], dsend.at[k], drecv.at[k])

    def snap_cols(p):
        return snap.at[:, pl.ds(pl.multiple_of(p * cols, cols), cols)]

    def w_slot(s):
        return RowRelay(row, lambda q: w_all.at[s, q], wsend.at[s], wrecv.at[s])

    def rows_of(size, part):
        return pl.ds(pl.multiple_of(part * (size // ng), size // ng), size // ng)

    def enc_part(s, part):
        return enc_all.at[s, rows_of(cols, part)]

    def w_part(s, part):
        return w_all.at[s, r, rows_of(weight.shape[1], part)]

    def block_part(s, part):
        return block_all.at[s, rows_of(block.shape[0], part)]

    def shards(step, act):
        for way in (1, -1):
            s = d - way * step

            @pl.when((s >= 0) & (s < dp))
            def _():
                act(s)

    def w_over_row(s):
        g_w.wait_recv(s)
        w_slot(s).start()

    def w_arrived(step):
        x_w.forward(step)
        shards(step, g_w.start)
        shards(step, w_over_row)

    def enc_arrived(step):
        x_enc.forward(step)
        shards(step, g_enc.start)

    def block_arrived(step):
        x_block.forward(step)
        shards(step, g_block.start)

    x_enc = Chain("dp", dp, lambda s: enc_part(s, g), csend.at[0], crecv.at[0])
    x_w = Chain("dp", dp, lambda s: w_part(s, g), csend.at[1], crecv.at[1])
    x_block = Chain("dp", dp, lambda s: block_part(s, g), csend.at[2], crecv.at[2])
    g_enc = Spread(ng, enc_part, gsend.at[0], grecv.at[0])
    g_w = Spread(ng, w_part, gsend.at[1], grecv.at[1])
    g_block = Spread(ng, block_part, gsend.at[2], grecv.at[2])
    x_bias = over_dp(0, lambda p: bias, bias_all)
    x_snap = over_dp(1, snap_cols, snap_all)
    own_block = pltpu.make_async_copy(block, block_all.at[d], lsem.at[0])
    own_snap = pltpu.make_async_copy(snap_cols(d), snap_all.at[d], lsem.at[1])
    own_block.start()
    own_snap.start()
    enc_all[d] = enc[...]
    x_enc.start()
    w_all[d, r] = weight[r]
    x_w.start()
    w_slot(d).start()
    bias_all[d] = bias[...]
    x_bias.start()
    for step in range(1, dp - 1):
        enc_arrived(step)
        w_arrived(step)
    own_block.wait()
    x_block.start()
    x_snap.start()
    enc_arrived(dp - 1)
    for s in others:
        g_enc.wait_recv(s)
    part = jnp.zeros((batch, enc.shape[1]), F32)
    for s in range(dp):
        part += dot(snap[:, s * cols : (s + 1) * cols], enc_all[s])
    lat_part[r] = part
    x_lat = Exchange("row", row, lambda p: lat_part.at[r], lambda s: lat_part.at[s], rsend, rrecv)
    x_lat.start()
    w_arrived(dp - 1)
    x_lat.wait_recv()
    total = lat_part[0]
    for s in range(1, row):
        total += lat_part[s]
    latent_b = total.astype(BF16)
    lat_all[d] = latent_b
    x_latb = over_dp(2, lambda p: lat_all.at[d], lat_all)
    x_latb.start()
    if dp > 2:
        block_arrived(1)
    x_bias.wait_recv()
    lines = lax.broadcasted_iota(jnp.int32, (bias.shape[0], batch), 0)

    def pre_of(s, q):
        pick = jnp.where(lines == q, 1.0, 0.0).astype(BF16)
        return dot(w_all[s, q], lat_all[d], 1, 1) + dot(bias_all[s], pick, 0, 0)

    for s in range(dp):
        pre[s] = pre_of(s, r)
    for s in range(dp):
        w_slot(s).forward()
    for step in range(2, dp - 1):
        block_arrived(step)

    def hid_of(s, _):
        w_slot(s).wait_recv()
        for q in range(row):
            hid[s, q] = jax.nn.silu(pre_of(s, q)).astype(BF16)
        return 0

    lax.fori_loop(0, dp, hid_of, 0)
    own_snap.wait()
    block_arrived(dp - 1)
    for s in others:
        g_block.wait_recv(s)
    for x in (x_latb, x_snap):
        x.wait_recv()
    for x in (x_enc, x_bias, x_w, x_block, x_snap, x_lat, x_latb):
        x.wait_send()
    for s in others:
        for x in (g_enc, g_w, g_block):
            x.wait_send(s)
    for s in range(dp):
        w_slot(s).wait_send()


def decode_kernel(scale, ids, counts, hid, block, snap, mis_ref, adj_ref, adj):
    tiles, slots, blk, _ = block.shape
    adj[...] = jnp.zeros_like(adj)

    def tile(t, _):
        count = counts[t]
        out = jnp.zeros((snap.shape[0], blk), F32)
        for k in range(slots):
            live = (k < count).astype(F32)
            out += dot(hid[ids[t, k]], block[t, k], 0, 0) * live
        here = snap[:, pl.ds(pl.multiple_of(t * blk, blk), blk)].astype(F32)
        misfit = ((out - here) * scale).astype(BF16)
        mis_ref[t] = misfit
        for k in range(slots):
            live = (k < count).astype(F32)
            adj[ids[t, k]] += dot(block[t, k], misfit, 1, 1) * live
        return 0

    lax.fori_loop(0, tiles, tile, 0)
    adj_ref[...] = adj[...].astype(BF16)


def block_grad_kernel(ids, counts, w, bias, lat, mis, grad):
    own, slots, blk, _ = grad.shape
    dp = mis.shape[0]
    ones = jnp.ones((bias.shape[1], mis.shape[2]), BF16)

    def slot(k, _):
        for t in range(own):
            j = ids[t, k]
            live = (k < counts[t]).astype(F32)
            shift = dot(bias[j], ones, 0, 0)
            o = jnp.zeros((blk, blk), F32)
            for s in range(dp):
                h = jax.nn.silu(dot(w[j], lat[s], 1, 1) + shift).astype(BF16)
                o += dot(h, mis[s, t])
            grad[t, k] = o * live
        return 0

    lax.fori_loop(0, slots, slot, 0)


def backward_kernel(
    row, dp, adj, mis, pre, lat_all, w_all, snap_all,
    wgrad, bgrad, enc_grad, mis_all,
    adj_all, pg, pg_all, lg_part, lg_all,
    dsend, drecv, rsend, rrecv, wsend, wrecv,
):
    r, d = lax.axis_index("row"), lax.axis_index("dp")
    greet({"row": row, "dp": dp})

    def over_dp(k, src_of, dst):
        return Exchange("dp", dp, src_of, lambda s: dst.at[s], dsend.at[k], drecv.at[k])

    def over_row(k, src_of, dst):
        return Exchange("row", row, src_of, lambda s: dst.at[s], rsend.at[k], rrecv.at[k])

    x_adj = over_row(0, lambda p: adj.at[:, p], adj_all)
    x_adj.start()
    x_mis = over_dp(0, lambda p: mis.at[p], mis_all)
    x_mis.start()
    adj_all[r] = adj[:, r]
    mis_all[d] = mis[d]
    x_adj.wait_recv()
    part = jnp.zeros((mis.shape[2], lat_all.shape[2]), F32)
    for s in range(dp):
        a = adj_all[0, s].astype(F32)
        for q in range(1, row):
            a += adj_all[q, s].astype(F32)
        v = pre[s]
        sigma = jax.nn.sigmoid(v)
        g = (a * (sigma * (1.0 + v * (1.0 - sigma)))).astype(BF16)
        pg[s] = g
    x_pg = over_dp(1, lambda p: pg.at[p], pg_all)
    x_pg.start()
    for s in range(dp):
        part += dot(pg[s], w_all[s, r], 0, 0)
    pg_all[d] = pg[d]
    lg_part[r] = part
    x_lg = over_row(1, lambda p: lg_part.at[r], lg_part)
    x_lg.start()
    x_lg.wait_recv()
    total = lg_part[0]
    for s in range(1, row):
        total += lg_part[s]
    lg_all[d] = total.astype(BF16)
    x_lgb = over_dp(2, lambda p: lg_all.at[d], lg_all)
    x_lgb.start()
    x_pg.wait_recv()
    w = jnp.zeros(wgrad.shape[1:], F32)
    b = jnp.zeros(bgrad.shape[1:], F32)
    ones = jnp.ones((bgrad.shape[1], mis.shape[2]), BF16)
    for s in range(dp):
        w += dot(pg_all[s], lat_all[s])
    wgrad[r] = w.astype(BF16)
    x_w = RowRelay(row, lambda q: wgrad.at[q], wsend, wrecv)
    x_w.start()
    for s in range(dp):
        b += dot(ones, pg_all[s], 1, 1)
    bgrad[r] = b
    x_b = over_row(2, lambda p: bgrad.at[r], bgrad)
    x_b.start()
    x_lgb.wait_recv()
    e = dot(snap_all[0], lg_all[0], 0, 0)
    for s in range(1, dp):
        e += dot(snap_all[s], lg_all[s], 0, 0)
    enc_grad[...] = e
    x_w.forward()
    x_mis.wait_recv()
    x_b.wait_recv()
    x_w.wait_recv()
    for x in (x_adj, x_mis, x_lg, x_pg, x_lgb, x_w, x_b):
        x.wait_send()


def on_device(
    ng, row, dp, snapshots, enc_weight, hidden_weight, hidden_bias, block_weight, block_ids, block_counts
):
    batch = snapshots.shape[0]
    own, slots, blk = block_weight.shape[:3]
    latent = enc_weight.shape[2]
    shard = hidden_weight.shape[0]
    part = shard // row
    tiles = own * dp
    cols = own * blk
    vmem = pl.BlockSpec(memory_space=pltpu.VMEM)
    smem = pl.BlockSpec(memory_space=pltpu.SMEM)
    dma = pltpu.SemaphoreType.DMA
    sds = jax.ShapeDtypeStruct
    bias = jnp.pad(hidden_bias.reshape(row, part), ((0, -row % 16), (0, 0)))
    hid, pre, lat_all, block_all, w_all, snap_all, bias_all = pl.pallas_call(
        functools.partial(forward_kernel, ng, row, dp),
        out_shape=(
            sds((dp, row, part, batch), BF16),
            sds((dp, part, batch), F32),
            sds((dp, batch, latent), BF16),
            sds((dp, own, slots, blk, blk), BF16),
            sds((dp, row, part, latent), BF16),
            sds((dp, batch, cols), BF16),
            sds((dp, *bias.shape), BF16),
        ),
        in_specs=[vmem] * 5,
        out_specs=[vmem] * 7,
        scratch_shapes=[
            pltpu.VMEM((dp, cols, latent), BF16),
            pltpu.VMEM((row, batch, latent), F32),
            dma((3, dp)), dma((3, dp)), dma((3, dp + 1)), dma((3, dp)), dma((row,)), dma((row,)),
            dma((dp, 2 * row)), dma((dp, row)),
            dma((3, dp * ng)), dma((3, dp * ng)), dma((2,)),
        ],
        compiler_params=pltpu.CompilerParams(
            collective_id=0, has_side_effects=True, vmem_limit_bytes=VMEM_LIMIT
        ),
        name="forward",
    )(
        snapshots,
        enc_weight.reshape(cols, latent),
        hidden_weight.reshape(row, part, latent),
        bias,
        block_weight,
    )
    nblocks = dp * shard // blk
    scale = 1.0 / math.sqrt(batch * dp)
    misfit, adj = pl.pallas_call(
        functools.partial(decode_kernel, scale),
        out_shape=(
            sds((tiles, batch, blk), BF16),
            sds((nblocks, blk, batch), BF16),
        ),
        in_specs=[smem, smem, vmem, vmem, vmem],
        out_specs=[vmem] * 2,
        scratch_shapes=[pltpu.VMEM((nblocks, blk, batch), F32)],
        compiler_params=pltpu.CompilerParams(vmem_limit_bytes=VMEM_LIMIT),
        name="decode",
    )(
        block_ids,
        block_counts,
        hid.reshape(nblocks, blk, batch),
        block_all.reshape(tiles, slots, blk, blk),
        snapshots,
    )
    weight_grad, bias_grad, enc_grad, mis_all = pl.pallas_call(
        functools.partial(backward_kernel, row, dp),
        out_shape=(
            sds((row, part, latent), BF16),
            sds((row, 8, part), F32),
            sds((cols, latent), F32),
            sds((dp, own, batch, blk), BF16),
        ),
        in_specs=[vmem] * 6,
        out_specs=[vmem] * 4,
        scratch_shapes=[
            pltpu.VMEM((row, dp, part, batch), BF16),
            pltpu.VMEM((dp, part, batch), BF16),
            pltpu.VMEM((dp, part, batch), BF16),
            pltpu.VMEM((row, batch, latent), F32),
            pltpu.VMEM((dp, batch, latent), BF16),
            dma((3, dp)), dma((3, dp)), dma((3, row)), dma((3, row)), dma((2 * row,)), dma((row,)),
        ],
        compiler_params=pltpu.CompilerParams(
            collective_id=1, has_side_effects=True, vmem_limit_bytes=VMEM_LIMIT
        ),
        name="backward",
    )(
        adj.reshape(dp, row, part, batch),
        misfit.reshape(dp, own, batch, blk),
        pre,
        lat_all,
        w_all,
        snap_all,
    )
    first = lax.axis_index("dp") * own
    bias_lines = bias_all[:, :row].reshape(nblocks, 1, blk)
    block_grad = pl.pallas_call(
        block_grad_kernel,
        out_shape=sds((own, slots, blk, blk), F32),
        in_specs=[smem, smem, vmem, vmem, vmem, vmem],
        out_specs=vmem,
        compiler_params=pltpu.CompilerParams(vmem_limit_bytes=VMEM_LIMIT),
        name="block_grad",
    )(
        lax.dynamic_slice_in_dim(block_ids, first, own),
        lax.dynamic_slice_in_dim(block_counts, first, own),
        w_all.reshape(nblocks, blk, latent),
        jnp.pad(bias_lines, ((0, 0), (0, 15), (0, 0))),
        lat_all,
        mis_all,
    )
    return (
        enc_grad.reshape(own, blk, latent),
        weight_grad.reshape(shard, latent).astype(F32),
        bias_grad[:, 0, :].reshape(shard),
        block_grad,
    )


def solution(mesh):
    in_specs = (
        P(("groups", "dp"), "row"),
        P(("row", "dp"), None, None),
        P("dp", None),
        P("dp"),
        P(("row", "dp"), None, None, None),
        P("row", None),
        P("row"),
    )
    out_specs = (
        P(("groups", "row", "dp"), None, None),
        P(("groups", "dp"), None),
        P(("groups", "dp")),
        P(("groups", "row", "dp"), None, None, None),
    )
    return jax.shard_map(
        functools.partial(on_device, mesh.shape["groups"], mesh.shape["row"], mesh.shape["dp"]),
        mesh=mesh, in_specs=in_specs, out_specs=out_specs, check_vma=False,
    )
```

```python
import functools
import math

import jax
import jax.numpy as jnp
from jax import lax
from jax.experimental import pallas as pl
from jax.experimental.pallas import tpu as pltpu
from jax.sharding import PartitionSpec as P

MESH = pl.DeviceIdType.MESH
F32 = jnp.float32
BF16 = jnp.bfloat16
VMEM_LIMIT = 56 * 1024 * 1024


def dot(a, b, ca=1, cb=0):
    return lax.dot_general(a, b, (((ca,), (cb,)), ((), ())), preferred_element_type=F32)


def greet(sizes):
    barrier = pltpu.get_barrier_semaphore()
    total = 0
    for axis, n in sizes.items():
        me = lax.axis_index(axis)
        for i in range(1, n):
            pl.semaphore_signal(
                barrier, inc=1, device_id={axis: lax.rem(me + i, n)}, device_id_type=MESH
            )
        total += n - 1
    pl.semaphore_wait(barrier, total)


class Exchange:
    def __init__(self, axis, n, src_of, dst_of, send, recv):
        self.axis, self.n, self.src_of, self.dst_of = axis, n, src_of, dst_of
        self.send, self.recv = send, recv
        self.me = lax.axis_index(axis)

    def copy(self, peer, slot):
        return pltpu.make_async_remote_copy(
            src_ref=self.src_of(peer),
            dst_ref=self.dst_of(slot),
            send_sem=self.send.at[peer],
            recv_sem=self.recv.at[slot],
            device_id={self.axis: peer},
            device_id_type=MESH,
        )

    def start(self):
        for i in range(1, self.n):
            self.copy(lax.rem(self.me + i, self.n), self.me).start()

    def wait_recv(self):
        for i in range(1, self.n):
            peer = lax.rem(self.me + i, self.n)
            self.copy(peer, peer).wait_recv()

    def wait_send(self):
        for i in range(1, self.n):
            self.copy(lax.rem(self.me + i, self.n), self.me).wait_send()


class Chain:
    def __init__(self, axis, n, dst_of, send, recv):
        self.axis, self.n, self.dst_of = axis, n, dst_of
        self.send, self.recv = send, recv
        self.me = lax.axis_index(axis)

    def copy(self, slot, way, sem):
        return pltpu.make_async_remote_copy(
            src_ref=self.dst_of(slot),
            dst_ref=self.dst_of(slot),
            send_sem=self.send.at[sem],
            recv_sem=self.recv.at[slot],
            device_id={self.axis: self.me + way},
            device_id_type=MESH,
        )

    def each(self, step, act):
        me, n = self.me, self.n
        for way in (1, -1):
            slot = me - way * step
            sem = slot if step or way == 1 else n
            there, held = me + way, slot
            ok = (there >= 0) & (there < n) & (held >= 0) & (held < n)

            @pl.when(ok)
            def _():
                act(self.copy(slot, way, sem))

    def arrived(self, step):
        for way in (1, -1):
            slot = self.me - way * step

            @pl.when((slot >= 0) & (slot < self.n))
            def _():
                self.copy(slot, -way, slot).wait_recv()

    def start(self):
        self.each(0, lambda c: c.start())

    def forward(self, step):
        self.arrived(step)
        self.each(step, lambda c: c.start())

    def wait_send(self):
        for step in range(self.n - 1):
            self.each(step, lambda c: c.wait_send())


class Spread:
    def __init__(self, ng, part_of, send, recv):
        self.ng, self.part_of, self.send, self.recv = ng, part_of, send, recv
        self.me = lax.axis_index("groups")
        self.peers = [lax.rem(self.me + i, ng) for i in range(1, ng)]

    def copy(self, slot, part, peer):
        return pltpu.make_async_remote_copy(
            src_ref=self.part_of(slot, part),
            dst_ref=self.part_of(slot, part),
            send_sem=self.send.at[slot * self.ng + peer],
            recv_sem=self.recv.at[slot * self.ng + part],
            device_id={"groups": peer},
            device_id_type=MESH,
        )

    def start(self, slot):
        for p in self.peers:
            self.copy(slot, self.me, p).start()

    def wait_recv(self, slot):
        for p in self.peers:
            self.copy(slot, p, p).wait_recv()

    def wait_send(self, slot):
        for p in self.peers:
            self.copy(slot, self.me, p).wait_send()


class RowRelay:
    def __init__(self, row, dst_of, send, recv):
        self.row, self.dst_of, self.send, self.recv = row, dst_of, send, recv
        self.me = lax.axis_index("row")
        self.sib = self.me + 1 - 2 * lax.rem(self.me, 2)
        self.peers = [lax.rem(self.me + 2 * i, row) for i in range(1, row // 2)]

    def copy(self, slot, to, sem):
        return pltpu.make_async_remote_copy(
            src_ref=self.dst_of(slot),
            dst_ref=self.dst_of(slot),
            send_sem=self.send.at[sem],
            recv_sem=self.recv.at[slot],
            device_id={"row": to},
            device_id_type=MESH,
        )

    def start(self):
        for p in self.peers:
            self.copy(self.me, p, p).start()
        self.copy(self.me, self.sib, self.sib).start()

    def forward(self):
        for p in self.peers:
            self.copy(p, p, p).wait_recv()
            self.copy(p, self.sib, self.row + p).start()

    def wait_recv(self):
        for p in [self.me, *self.peers]:
            slot = p + 1 - 2 * lax.rem(p, 2)
            self.copy(slot, self.sib, slot).wait_recv()

    def wait_send(self):
        for p in self.peers:
            self.copy(self.me, p, p).wait_send()
            self.copy(p, self.sib, self.row + p).wait_send()
        self.copy(self.me, self.sib, self.sib).wait_send()


def forward_kernel(
    ng, row, dp, snap, enc, weight, bias, block,
    hid, pre, lat_all, block_all, w_all, snap_all, bias_all,
    enc_all, lat_part, dsend, drecv, csend, crecv, rsend, rrecv, wsend, wrecv, gsend, grecv, lsem,
):
    r, d = lax.axis_index("row"), lax.axis_index("dp")
    cols = snap.shape[1] // dp
    batch = snap.shape[0]
    g = lax.axis_index("groups")
    others = [lax.rem(d + i, dp) for i in range(1, dp)]
    greet({"groups": ng, "row": row, "dp": dp})

    def over_dp(k, src_of, dst):
        return Exchange("dp", dp, src_of, lambda s: dst.at[s], dsend.at[k], drecv.at[k])

    def snap_cols(p):
        return snap.at[:, pl.ds(pl.multiple_of(p * cols, cols), cols)]

    def w_slot(s):
        return RowRelay(row, lambda q: w_all.at[s, q], wsend.at[s], wrecv.at[s])

    def rows_of(size, part):
        return pl.ds(pl.multiple_of(part * (size // ng), size // ng), size // ng)

    def enc_part(s, part):
        return enc_all.at[s, rows_of(cols, part)]

    def w_part(s, part):
        return w_all.at[s, r, rows_of(weight.shape[1], part)]

    def block_part(s, part):
        return block_all.at[s, rows_of(block.shape[0], part)]

    def shards(step, act):
        for way in (1, -1):
            s = d - way * step

            @pl.when((s >= 0) & (s < dp))
            def _():
                act(s)

    def w_over_row(s):
        g_w.wait_recv(s)
        w_slot(s).start()

    def w_arrived(step):
        x_w.forward(step)
        shards(step, g_w.start)
        shards(step, w_over_row)

    def enc_arrived(step):
        x_enc.forward(step)
        shards(step, g_enc.start)

    def block_arrived(step):
        x_block.forward(step)
        shards(step, g_block.start)

    x_enc = Chain("dp", dp, lambda s: enc_part(s, g), csend.at[0], crecv.at[0])
    x_w = Chain("dp", dp, lambda s: w_part(s, g), csend.at[1], crecv.at[1])
    x_block = Chain("dp", dp, lambda s: block_part(s, g), csend.at[2], crecv.at[2])
    g_enc = Spread(ng, enc_part, gsend.at[0], grecv.at[0])
    g_w = Spread(ng, w_part, gsend.at[1], grecv.at[1])
    g_block = Spread(ng, block_part, gsend.at[2], grecv.at[2])
    x_bias = over_dp(0, lambda p: bias, bias_all)
    x_snap = over_dp(1, snap_cols, snap_all)
    own_block = pltpu.make_async_copy(block, block_all.at[d], lsem.at[0])
    own_snap = pltpu.make_async_copy(snap_cols(d), snap_all.at[d], lsem.at[1])
    own_block.start()
    own_snap.start()
    enc_all[d] = enc[...]
    x_enc.start()
    w_all[d, r] = weight[r]
    x_w.start()
    w_slot(d).start()
    bias_all[d] = bias[...]
    x_bias.start()
    own_block.wait()
    x_block.start()
    for step in range(1, dp - 1):
        enc_arrived(step)
        w_arrived(step)
    enc_arrived(dp - 1)
    for s in others:
        g_enc.wait_recv(s)
    part = jnp.zeros((batch, enc.shape[1]), F32)
    for s in range(dp):
        part += dot(snap[:, s * cols : (s + 1) * cols], enc_all[s])
    lat_part[r] = part
    x_lat = Exchange("row", row, lambda p: lat_part.at[r], lambda s: lat_part.at[s], rsend, rrecv)
    x_lat.start()
    w_arrived(dp - 1)
    if dp > 2:
        block_arrived(1)
    x_lat.wait_recv()
    total = lat_part[0]
    for s in range(1, row):
        total += lat_part[s]
    latent_b = total.astype(BF16)
    lat_all[d] = latent_b
    x_latb = over_dp(2, lambda p: lat_all.at[d], lat_all)
    x_latb.start()
    for s in range(dp):
        w_slot(s).forward()
    for step in range(2, dp - 1):
        block_arrived(step)
    x_snap.start()
    x_bias.wait_recv()
    lines = lax.broadcasted_iota(jnp.int32, (bias.shape[0], batch), 0)

    def pre_of(s, q):
        pick = jnp.where(lines == q, 1.0, 0.0).astype(BF16)
        return dot(w_all[s, q], lat_all[d], 1, 1) + dot(bias_all[s], pick, 0, 0)

    for s in range(dp):
        pre[s] = pre_of(s, r)

    def hid_of(s, _):
        w_slot(s).wait_recv()
        for q in range(row):
            hid[s, q] = jax.nn.silu(pre_of(s, q)).astype(BF16)
        return 0

    lax.fori_loop(0, dp, hid_of, 0)
    own_snap.wait()
    block_arrived(dp - 1)
    for s in others:
        g_block.wait_recv(s)
    for x in (x_latb, x_snap):
        x.wait_recv()
    for x in (x_enc, x_bias, x_w, x_block, x_snap, x_lat, x_latb):
        x.wait_send()
    for s in others:
        for x in (g_enc, g_w, g_block):
            x.wait_send(s)
    for s in range(dp):
        w_slot(s).wait_send()


def decode_kernel(scale, ids, counts, hid, block, snap, mis_ref, adj_ref, adj):
    tiles, slots, blk, _ = block.shape
    adj[...] = jnp.zeros_like(adj)

    def tile(t, _):
        count = counts[t]
        out = jnp.zeros((snap.shape[0], blk), F32)
        for k in range(slots):
            live = (k < count).astype(F32)
            out += dot(hid[ids[t, k]], block[t, k], 0, 0) * live
        here = snap[:, pl.ds(pl.multiple_of(t * blk, blk), blk)].astype(F32)
        misfit = ((out - here) * scale).astype(BF16)
        mis_ref[t] = misfit
        for k in range(slots):
            live = (k < count).astype(F32)
            adj[ids[t, k]] += dot(block[t, k], misfit, 1, 1) * live
        return 0

    lax.fori_loop(0, tiles, tile, 0)
    adj_ref[...] = adj[...].astype(BF16)


def block_grad_kernel(ids, counts, w, bias, lat, mis, grad):
    own, slots, blk, _ = grad.shape
    dp = mis.shape[0]
    ones = jnp.ones((bias.shape[1], mis.shape[2]), BF16)

    def slot(k, _):
        for t in range(own):
            j = ids[t, k]
            live = (k < counts[t]).astype(F32)
            shift = dot(bias[j], ones, 0, 0)
            o = jnp.zeros((blk, blk), F32)
            for s in range(dp):
                h = jax.nn.silu(dot(w[j], lat[s], 1, 1) + shift).astype(BF16)
                o += dot(h, mis[s, t])
            grad[t, k] = o * live
        return 0

    lax.fori_loop(0, slots, slot, 0)


def backward_kernel(
    row, dp, adj, mis, pre, lat_all, w_all, snap_all,
    wgrad, bgrad, enc_grad, mis_all,
    adj_all, pg, pg_all, lg_part, lg_all,
    dsend, drecv, rsend, rrecv, wsend, wrecv,
):
    r, d = lax.axis_index("row"), lax.axis_index("dp")
    greet({"row": row, "dp": dp})

    def over_dp(k, src_of, dst):
        return Exchange("dp", dp, src_of, lambda s: dst.at[s], dsend.at[k], drecv.at[k])

    def over_row(k, src_of, dst):
        return Exchange("row", row, src_of, lambda s: dst.at[s], rsend.at[k], rrecv.at[k])

    x_adj = over_row(0, lambda p: adj.at[:, p], adj_all)
    x_adj.start()
    x_mis = over_dp(0, lambda p: mis.at[p], mis_all)
    x_mis.start()
    adj_all[r] = adj[:, r]
    mis_all[d] = mis[d]
    x_adj.wait_recv()
    part = jnp.zeros((mis.shape[2], lat_all.shape[2]), F32)
    for s in range(dp):
        a = adj_all[0, s].astype(F32)
        for q in range(1, row):
            a += adj_all[q, s].astype(F32)
        v = pre[s]
        sigma = jax.nn.sigmoid(v)
        g = (a * (sigma * (1.0 + v * (1.0 - sigma)))).astype(BF16)
        pg[s] = g
    x_pg = over_dp(1, lambda p: pg.at[p], pg_all)
    x_pg.start()
    for s in range(dp):
        part += dot(pg[s], w_all[s, r], 0, 0)
    pg_all[d] = pg[d]
    lg_part[r] = part
    x_lg = over_row(1, lambda p: lg_part.at[r], lg_part)
    x_lg.start()
    x_lg.wait_recv()
    total = lg_part[0]
    for s in range(1, row):
        total += lg_part[s]
    lg_all[d] = total.astype(BF16)
    x_lgb = over_dp(2, lambda p: lg_all.at[d], lg_all)
    x_lgb.start()
    x_pg.wait_recv()
    w = jnp.zeros(wgrad.shape[1:], F32)
    b = jnp.zeros(bgrad.shape[1:], F32)
    ones = jnp.ones((bgrad.shape[1], mis.shape[2]), BF16)
    for s in range(dp):
        w += dot(pg_all[s], lat_all[s])
    wgrad[r] = w.astype(BF16)
    x_w = RowRelay(row, lambda q: wgrad.at[q], wsend, wrecv)
    x_w.start()
    for s in range(dp):
        b += dot(ones, pg_all[s], 1, 1)
    bgrad[r] = b
    x_b = over_row(2, lambda p: bgrad.at[r], bgrad)
    x_b.start()
    x_lgb.wait_recv()
    e = dot(snap_all[0], lg_all[0], 0, 0)
    for s in range(1, dp):
        e += dot(snap_all[s], lg_all[s], 0, 0)
    enc_grad[...] = e
    x_w.forward()
    x_mis.wait_recv()
    x_b.wait_recv()
    x_w.wait_recv()
    for x in (x_adj, x_mis, x_lg, x_pg, x_lgb, x_w, x_b):
        x.wait_send()


def on_device(
    ng, row, dp, snapshots, enc_weight, hidden_weight, hidden_bias, block_weight, block_ids, block_counts
):
    batch = snapshots.shape[0]
    own, slots, blk = block_weight.shape[:3]
    latent = enc_weight.shape[2]
    shard = hidden_weight.shape[0]
    part = shard // row
    tiles = own * dp
    cols = own * blk
    vmem = pl.BlockSpec(memory_space=pltpu.VMEM)
    smem = pl.BlockSpec(memory_space=pltpu.SMEM)
    dma = pltpu.SemaphoreType.DMA
    sds = jax.ShapeDtypeStruct
    bias = jnp.pad(hidden_bias.reshape(row, part), ((0, -row % 16), (0, 0)))
    hid, pre, lat_all, block_all, w_all, snap_all, bias_all = pl.pallas_call(
        functools.partial(forward_kernel, ng, row, dp),
        out_shape=(
            sds((dp, row, part, batch), BF16),
            sds((dp, part, batch), F32),
            sds((dp, batch, latent), BF16),
            sds((dp, own, slots, blk, blk), BF16),
            sds((dp, row, part, latent), BF16),
            sds((dp, batch, cols), BF16),
            sds((dp, *bias.shape), BF16),
        ),
        in_specs=[vmem] * 5,
        out_specs=[vmem] * 7,
        scratch_shapes=[
            pltpu.VMEM((dp, cols, latent), BF16),
            pltpu.VMEM((row, batch, latent), F32),
            dma((3, dp)), dma((3, dp)), dma((3, dp + 1)), dma((3, dp)), dma((row,)), dma((row,)),
            dma((dp, 2 * row)), dma((dp, row)),
            dma((3, dp * ng)), dma((3, dp * ng)), dma((2,)),
        ],
        compiler_params=pltpu.CompilerParams(
            collective_id=0, has_side_effects=True, vmem_limit_bytes=VMEM_LIMIT
        ),
        name="forward",
    )(
        snapshots,
        enc_weight.reshape(cols, latent),
        hidden_weight.reshape(row, part, latent),
        bias,
        block_weight,
    )
    nblocks = dp * shard // blk
    scale = 1.0 / math.sqrt(batch * dp)
    misfit, adj = pl.pallas_call(
        functools.partial(decode_kernel, scale),
        out_shape=(
            sds((tiles, batch, blk), BF16),
            sds((nblocks, blk, batch), BF16),
        ),
        in_specs=[smem, smem, vmem, vmem, vmem],
        out_specs=[vmem] * 2,
        scratch_shapes=[pltpu.VMEM((nblocks, blk, batch), F32)],
        compiler_params=pltpu.CompilerParams(vmem_limit_bytes=VMEM_LIMIT),
        name="decode",
    )(
        block_ids,
        block_counts,
        hid.reshape(nblocks, blk, batch),
        block_all.reshape(tiles, slots, blk, blk),
        snapshots,
    )
    weight_grad, bias_grad, enc_grad, mis_all = pl.pallas_call(
        functools.partial(backward_kernel, row, dp),
        out_shape=(
            sds((row, part, latent), BF16),
            sds((row, 8, part), F32),
            sds((cols, latent), F32),
            sds((dp, own, batch, blk), BF16),
        ),
        in_specs=[vmem] * 6,
        out_specs=[vmem] * 4,
        scratch_shapes=[
            pltpu.VMEM((row, dp, part, batch), BF16),
            pltpu.VMEM((dp, part, batch), BF16),
            pltpu.VMEM((dp, part, batch), BF16),
            pltpu.VMEM((row, batch, latent), F32),
            pltpu.VMEM((dp, batch, latent), BF16),
            dma((3, dp)), dma((3, dp)), dma((3, row)), dma((3, row)), dma((2 * row,)), dma((row,)),
        ],
        compiler_params=pltpu.CompilerParams(
            collective_id=1, has_side_effects=True, vmem_limit_bytes=VMEM_LIMIT
        ),
        name="backward",
    )(
        adj.reshape(dp, row, part, batch),
        misfit.reshape(dp, own, batch, blk),
        pre,
        lat_all,
        w_all,
        snap_all,
    )
    first = lax.axis_index("dp") * own
    bias_lines = bias_all[:, :row].reshape(nblocks, 1, blk)
    block_grad = pl.pallas_call(
        block_grad_kernel,
        out_shape=sds((own, slots, blk, blk), F32),
        in_specs=[smem, smem, vmem, vmem, vmem, vmem],
        out_specs=vmem,
        compiler_params=pltpu.CompilerParams(vmem_limit_bytes=VMEM_LIMIT),
        name="block_grad",
    )(
        lax.dynamic_slice_in_dim(block_ids, first, own),
        lax.dynamic_slice_in_dim(block_counts, first, own),
        w_all.reshape(nblocks, blk, latent),
        jnp.pad(bias_lines, ((0, 0), (0, 15), (0, 0))),
        lat_all,
        mis_all,
    )
    return (
        enc_grad.reshape(own, blk, latent),
        weight_grad.reshape(shard, latent).astype(F32),
        bias_grad[:, 0, :].reshape(shard),
        block_grad,
    )


def solution(mesh):
    in_specs = (
        P(("groups", "dp"), "row"),
        P(("row", "dp"), None, None),
        P("dp", None),
        P("dp"),
        P(("row", "dp"), None, None, None),
        P("row", None),
        P("row"),
    )
    out_specs = (
        P(("groups", "row", "dp"), None, None),
        P(("groups", "dp"), None),
        P(("groups", "dp")),
        P(("groups", "row", "dp"), None, None, None),
    )
    return jax.shard_map(
        functools.partial(on_device, mesh.shape["groups"], mesh.shape["row"], mesh.shape["dp"]),
        mesh=mesh, in_specs=in_specs, out_specs=out_specs, check_vma=False,
    )
```

```python
import functools
import math

import jax
import jax.numpy as jnp
from jax import lax
from jax.experimental import pallas as pl
from jax.experimental.pallas import tpu as pltpu
from jax.sharding import PartitionSpec as P

MESH = pl.DeviceIdType.MESH
F32 = jnp.float32
BF16 = jnp.bfloat16
VMEM_LIMIT = 56 * 1024 * 1024


def dot(a, b, ca=1, cb=0):
    return lax.dot_general(a, b, (((ca,), (cb,)), ((), ())), preferred_element_type=F32)


def greet(sizes):
    barrier = pltpu.get_barrier_semaphore()
    total = 0
    for axis, n in sizes.items():
        me = lax.axis_index(axis)
        for i in range(1, n):
            pl.semaphore_signal(
                barrier, inc=1, device_id={axis: lax.rem(me + i, n)}, device_id_type=MESH
            )
        total += n - 1
    pl.semaphore_wait(barrier, total)


class Exchange:
    def __init__(self, axis, n, src_of, dst_of, send, recv):
        self.axis, self.n, self.src_of, self.dst_of = axis, n, src_of, dst_of
        self.send, self.recv = send, recv
        self.me = lax.axis_index(axis)

    def copy(self, peer, slot):
        return pltpu.make_async_remote_copy(
            src_ref=self.src_of(peer),
            dst_ref=self.dst_of(slot),
            send_sem=self.send.at[peer],
            recv_sem=self.recv.at[slot],
            device_id={self.axis: peer},
            device_id_type=MESH,
        )

    def start(self):
        for i in range(1, self.n):
            self.copy(lax.rem(self.me + i, self.n), self.me).start()

    def wait_recv(self):
        for i in range(1, self.n):
            peer = lax.rem(self.me + i, self.n)
            self.copy(peer, peer).wait_recv()

    def wait_send(self):
        for i in range(1, self.n):
            self.copy(lax.rem(self.me + i, self.n), self.me).wait_send()


class Chain:
    def __init__(self, axis, n, dst_of, send, recv):
        self.axis, self.n, self.dst_of = axis, n, dst_of
        self.send, self.recv = send, recv
        self.me = lax.axis_index(axis)

    def copy(self, slot, way, sem):
        return pltpu.make_async_remote_copy(
            src_ref=self.dst_of(slot),
            dst_ref=self.dst_of(slot),
            send_sem=self.send.at[sem],
            recv_sem=self.recv.at[slot],
            device_id={self.axis: self.me + way},
            device_id_type=MESH,
        )

    def each(self, step, act):
        me, n = self.me, self.n
        for way in (1, -1):
            slot = me - way * step
            sem = slot if step or way == 1 else n
            there, held = me + way, slot
            ok = (there >= 0) & (there < n) & (held >= 0) & (held < n)

            @pl.when(ok)
            def _():
                act(self.copy(slot, way, sem))

    def arrived(self, step):
        for way in (1, -1):
            slot = self.me - way * step

            @pl.when((slot >= 0) & (slot < self.n))
            def _():
                self.copy(slot, -way, slot).wait_recv()

    def start(self):
        self.each(0, lambda c: c.start())

    def forward(self, step):
        self.arrived(step)
        self.each(step, lambda c: c.start())

    def wait_send(self):
        for step in range(self.n - 1):
            self.each(step, lambda c: c.wait_send())


class Spread:
    def __init__(self, ng, part_of, send, recv):
        self.ng, self.part_of, self.send, self.recv = ng, part_of, send, recv
        self.me = lax.axis_index("groups")
        self.peers = [lax.rem(self.me + i, ng) for i in range(1, ng)]

    def copy(self, slot, part, peer):
        return pltpu.make_async_remote_copy(
            src_ref=self.part_of(slot, part),
            dst_ref=self.part_of(slot, part),
            send_sem=self.send.at[slot * self.ng + peer],
            recv_sem=self.recv.at[slot * self.ng + part],
            device_id={"groups": peer},
            device_id_type=MESH,
        )

    def start(self, slot):
        for p in self.peers:
            self.copy(slot, self.me, p).start()

    def wait_recv(self, slot):
        for p in self.peers:
            self.copy(slot, p, p).wait_recv()

    def wait_send(self, slot):
        for p in self.peers:
            self.copy(slot, self.me, p).wait_send()


class RowRelay:
    def __init__(self, row, dst_of, send, recv):
        self.row, self.dst_of, self.send, self.recv = row, dst_of, send, recv
        self.me = lax.axis_index("row")
        self.sib = self.me + 1 - 2 * lax.rem(self.me, 2)
        self.peers = [lax.rem(self.me + 2 * i, row) for i in range(1, row // 2)]

    def copy(self, slot, to, sem):
        return pltpu.make_async_remote_copy(
            src_ref=self.dst_of(slot),
            dst_ref=self.dst_of(slot),
            send_sem=self.send.at[sem],
            recv_sem=self.recv.at[slot],
            device_id={"row": to},
            device_id_type=MESH,
        )

    def start(self):
        for p in self.peers:
            self.copy(self.me, p, p).start()
        self.copy(self.me, self.sib, self.sib).start()

    def forward(self):
        for p in self.peers:
            self.copy(p, p, p).wait_recv()
            self.copy(p, self.sib, self.row + p).start()

    def wait_recv(self):
        for p in [self.me, *self.peers]:
            slot = p + 1 - 2 * lax.rem(p, 2)
            self.copy(slot, self.sib, slot).wait_recv()

    def wait_send(self):
        for p in self.peers:
            self.copy(self.me, p, p).wait_send()
            self.copy(p, self.sib, self.row + p).wait_send()
        self.copy(self.me, self.sib, self.sib).wait_send()


def forward_kernel(
    ng, row, dp, snap, enc, weight, bias, block,
    hid, pre, lat_all, block_all, w_all, snap_all, bias_all,
    enc_all, lat_part, dsend, drecv, csend, crecv, rsend, rrecv, wsend, wrecv, gsend, grecv, lsem,
):
    r, d = lax.axis_index("row"), lax.axis_index("dp")
    cols = snap.shape[1] // dp
    batch = snap.shape[0]
    g = lax.axis_index("groups")
    others = [lax.rem(d + i, dp) for i in range(1, dp)]
    greet({"groups": ng, "row": row, "dp": dp})

    def over_dp(k, src_of, dst):
        return Exchange("dp", dp, src_of, lambda s: dst.at[s], dsend.at[k], drecv.at[k])

    def snap_cols(p):
        return snap.at[:, pl.ds(pl.multiple_of(p * cols, cols), cols)]

    def w_slot(s):
        return RowRelay(row, lambda q: w_all.at[s, q], wsend.at[s], wrecv.at[s])

    def rows_of(size, part):
        return pl.ds(pl.multiple_of(part * (size // ng), size // ng), size // ng)

    def enc_part(s, part):
        return enc_all.at[s, rows_of(cols, part)]

    def w_part(s, part):
        return w_all.at[s, r, rows_of(weight.shape[1], part)]

    def block_part(s, part):
        return block_all.at[s, rows_of(block.shape[0], part)]

    def shards(step, act):
        for way in (1, -1):
            s = d - way * step

            @pl.when((s >= 0) & (s < dp))
            def _():
                act(s)

    def w_over_row(s):
        g_w.wait_recv(s)
        w_slot(s).start()

    def w_arrived(step):
        x_w.forward(step)
        shards(step, g_w.start)
        shards(step, w_over_row)

    def enc_arrived(step):
        x_enc.forward(step)
        shards(step, g_enc.start)

    def block_arrived(step):
        x_block.forward(step)
        shards(step, g_block.start)

    x_enc = Chain("dp", dp, lambda s: enc_part(s, g), csend.at[0], crecv.at[0])
    x_w = Chain("dp", dp, lambda s: w_part(s, g), csend.at[1], crecv.at[1])
    x_block = Chain("dp", dp, lambda s: block_part(s, g), csend.at[2], crecv.at[2])
    g_enc = Spread(ng, enc_part, gsend.at[0], grecv.at[0])
    g_w = Spread(ng, w_part, gsend.at[1], grecv.at[1])
    g_block = Spread(ng, block_part, gsend.at[2], grecv.at[2])
    x_bias = over_dp(0, lambda p: bias, bias_all)
    x_snap = over_dp(1, snap_cols, snap_all)
    own_block = pltpu.make_async_copy(block, block_all.at[d], lsem.at[0])
    own_snap = pltpu.make_async_copy(snap_cols(d), snap_all.at[d], lsem.at[1])
    own_block.start()
    own_snap.start()
    enc_all[d] = enc[...]
    x_enc.start()
    w_all[d, r] = weight[r]
    x_w.start()
    w_slot(d).start()
    bias_all[d] = bias[...]
    x_bias.start()
    own_block.wait()
    x_block.start()
    for step in range(1, dp - 1):
        enc_arrived(step)
        w_arrived(step)
    enc_arrived(dp - 1)
    for s in others:
        g_enc.wait_recv(s)
    part = jnp.zeros((batch, enc.shape[1]), F32)
    for s in range(dp):
        part += dot(snap[:, s * cols : (s + 1) * cols], enc_all[s])
    lat_part[r] = part
    x_lat = Exchange("row", row, lambda p: lat_part.at[r], lambda s: lat_part.at[s], rsend, rrecv)
    x_lat.start()
    w_arrived(dp - 1)
    if dp > 2:
        block_arrived(1)
    x_lat.wait_recv()
    total = lat_part[0]
    for s in range(1, row):
        total += lat_part[s]
    latent_b = total.astype(BF16)
    lat_all[d] = latent_b
    x_latb = over_dp(2, lambda p: lat_all.at[d], lat_all)
    x_latb.start()
    for s in range(dp):
        w_slot(s).forward()
    for step in range(2, dp - 1):
        block_arrived(step)
    x_snap.start()
    x_bias.wait_recv()
    lines = lax.broadcasted_iota(jnp.int32, (bias.shape[0], batch), 0)

    def pre_of(s, q):
        pick = jnp.where(lines == q, 1.0, 0.0).astype(BF16)
        return dot(w_all[s, q], lat_all[d], 1, 1) + dot(bias_all[s], pick, 0, 0)

    for s in range(dp):
        pre[s] = pre_of(s, r)

    def hid_of(s, _):
        w_slot(s).wait_recv()
        for q in range(row):
            hid[s, q] = jax.nn.silu(pre_of(s, q)).astype(BF16)
        return 0

    lax.fori_loop(0, dp, hid_of, 0)
    own_snap.wait()
    block_arrived(dp - 1)
    for s in others:
        g_block.wait_recv(s)
    for x in (x_latb, x_snap):
        x.wait_recv()
    for x in (x_enc, x_bias, x_w, x_block, x_snap, x_lat, x_latb):
        x.wait_send()
    for s in others:
        for x in (g_enc, g_w, g_block):
            x.wait_send(s)
    for s in range(dp):
        w_slot(s).wait_send()


def decode_kernel(scale, ids, counts, hid, block, snap, mis_ref, adj_ref, adj):
    tiles, slots, blk, _ = block.shape
    adj[...] = jnp.zeros_like(adj)

    def tile(t, _):
        count = counts[t]
        out = jnp.zeros((snap.shape[0], blk), F32)
        for k in range(slots):
            live = (k < count).astype(F32)
            out += dot(hid[ids[t, k]], block[t, k], 0, 0) * live
        here = snap[:, pl.ds(pl.multiple_of(t * blk, blk), blk)].astype(F32)
        misfit = ((out - here) * scale).astype(BF16)
        mis_ref[t] = misfit
        for k in range(slots):
            live = (k < count).astype(F32)
            adj[ids[t, k]] += dot(block[t, k], misfit, 1, 1) * live
        return 0

    lax.fori_loop(0, tiles, tile, 0)
    adj_ref[...] = adj[...].astype(BF16)


def block_grad_kernel(ids, counts, w, bias, lat, mis, grad):
    own, slots, blk, _ = grad.shape
    first = lax.axis_index("dp") * own
    dp = mis.shape[0]
    ones = jnp.ones((bias.shape[1], mis.shape[2]), BF16)

    def slot(k, _):
        for t in range(own):
            j = ids[first + t, k]
            live = (k < counts[first + t]).astype(F32)
            shift = dot(bias[j], ones, 0, 0)
            o = jnp.zeros((blk, blk), F32)
            for s in range(dp):
                h = jax.nn.silu(dot(w[j], lat[s], 1, 1) + shift).astype(BF16)
                o += dot(h, mis[s, t])
            grad[t, k] = o * live
        return 0

    lax.fori_loop(0, slots, slot, 0)


def backward_kernel(
    row, dp, adj, mis, pre, lat_all, w_all, snap_all,
    wgrad, bgrad, enc_grad, mis_all,
    sib_adj, pair, adj_all, pg, pg_all, lg_part, lg_all,
    dsend, drecv, rsend, rrecv, wsend, wrecv, asend, arecv, ssem,
):
    r, d = lax.axis_index("row"), lax.axis_index("dp")
    greet({"row": row, "dp": dp})

    def over_dp(k, src_of, dst):
        return Exchange("dp", dp, src_of, lambda s: dst.at[s], dsend.at[k], drecv.at[k])

    def over_row(k, src_of, dst):
        return Exchange("row", row, src_of, lambda s: dst.at[s], rsend.at[k], rrecv.at[k])

    y, c = lax.div(r, 2), lax.rem(r, 2)
    chips = row // 2
    far = [lax.rem(y + i, chips) for i in range(1, chips)]
    to_sib = pltpu.make_async_remote_copy(
        src_ref=adj.at[:, :, 1 - c],
        dst_ref=sib_adj,
        send_sem=ssem.at[0],
        recv_sem=ssem.at[1],
        device_id={"row": r + 1 - 2 * c},
        device_id_type=MESH,
    )
    to_sib.start()

    def to_chip(p, slot):
        return pltpu.make_async_remote_copy(
            src_ref=pair.at[p],
            dst_ref=adj_all.at[slot],
            send_sem=asend.at[p],
            recv_sem=arecv.at[slot],
            device_id={"row": 2 * p + c},
            device_id_type=MESH,
        )

    x_mis = over_dp(0, lambda p: mis.at[p], mis_all)
    x_mis.start()
    mis_all[d] = mis[d]
    to_sib.wait_recv()
    for p in far:
        for s in range(dp):
            both = adj[s, p, c].astype(F32) + sib_adj[s, p].astype(F32)
            pair[p, s] = both.astype(BF16)
        to_chip(p, y).start()
    for p in far:
        to_chip(p, p).wait_recv()
    part = jnp.zeros((mis.shape[2], lat_all.shape[2]), F32)
    for s in range(dp):
        a = adj[s, y, c].astype(F32) + sib_adj[s, y].astype(F32)
        for p in far:
            a += adj_all[p, s].astype(F32)
        v = pre[s]
        sigma = jax.nn.sigmoid(v)
        g = (a * (sigma * (1.0 + v * (1.0 - sigma)))).astype(BF16)
        pg[s] = g
    x_pg = over_dp(1, lambda p: pg.at[p], pg_all)
    x_pg.start()
    for s in range(dp):
        part += dot(pg[s], w_all[s, r], 0, 0)
    pg_all[d] = pg[d]
    lg_part[r] = part
    x_lg = over_row(1, lambda p: lg_part.at[r], lg_part)
    x_lg.start()
    x_lg.wait_recv()
    total = lg_part[0]
    for s in range(1, row):
        total += lg_part[s]
    lg_all[d] = total.astype(BF16)
    x_lgb = over_dp(2, lambda p: lg_all.at[d], lg_all)
    x_lgb.start()
    x_pg.wait_recv()
    w = jnp.zeros(wgrad.shape[1:], F32)
    b = jnp.zeros(bgrad.shape[1:], F32)
    ones = jnp.ones((bgrad.shape[1], mis.shape[2]), BF16)
    for s in range(dp):
        w += dot(pg_all[s], lat_all[s])
    wgrad[r] = w.astype(BF16)
    x_w = RowRelay(row, lambda q: wgrad.at[q], wsend, wrecv)
    x_w.start()
    for s in range(dp):
        b += dot(ones, pg_all[s], 1, 1)
    bgrad[r] = b
    x_b = over_row(2, lambda p: bgrad.at[r], bgrad)
    x_b.start()
    x_lgb.wait_recv()
    e = dot(snap_all[0], lg_all[0], 0, 0)
    for s in range(1, dp):
        e += dot(snap_all[s], lg_all[s], 0, 0)
    enc_grad[...] = e
    x_w.forward()
    x_mis.wait_recv()
    x_b.wait_recv()
    x_w.wait_recv()
    to_sib.wait_send()
    for p in far:
        to_chip(p, y).wait_send()
    for x in (x_mis, x_lg, x_pg, x_lgb, x_w, x_b):
        x.wait_send()


def on_device(
    ng, row, dp, snapshots, enc_weight, hidden_weight, hidden_bias, block_weight, block_ids, block_counts
):
    batch = snapshots.shape[0]
    own, slots, blk = block_weight.shape[:3]
    latent = enc_weight.shape[2]
    shard = hidden_weight.shape[0]
    part = shard // row
    tiles = own * dp
    cols = own * blk
    vmem = pl.BlockSpec(memory_space=pltpu.VMEM)
    smem = pl.BlockSpec(memory_space=pltpu.SMEM)
    dma = pltpu.SemaphoreType.DMA
    sds = jax.ShapeDtypeStruct
    bias = jnp.pad(hidden_bias.reshape(row, part), ((0, -row % 16), (0, 0)))
    hid, pre, lat_all, block_all, w_all, snap_all, bias_all = pl.pallas_call(
        functools.partial(forward_kernel, ng, row, dp),
        out_shape=(
            sds((dp, row, part, batch), BF16),
            sds((dp, part, batch), F32),
            sds((dp, batch, latent), BF16),
            sds((dp, own, slots, blk, blk), BF16),
            sds((dp, row, part, latent), BF16),
            sds((dp, batch, cols), BF16),
            sds((dp, *bias.shape), BF16),
        ),
        in_specs=[vmem] * 5,
        out_specs=[vmem] * 7,
        scratch_shapes=[
            pltpu.VMEM((dp, cols, latent), BF16),
            pltpu.VMEM((row, batch, latent), F32),
            dma((3, dp)), dma((3, dp)), dma((3, dp + 1)), dma((3, dp)), dma((row,)), dma((row,)),
            dma((dp, 2 * row)), dma((dp, row)),
            dma((3, dp * ng)), dma((3, dp * ng)), dma((2,)),
        ],
        compiler_params=pltpu.CompilerParams(
            collective_id=0, has_side_effects=True, vmem_limit_bytes=VMEM_LIMIT
        ),
        name="forward",
    )(
        snapshots,
        enc_weight.reshape(cols, latent),
        hidden_weight.reshape(row, part, latent),
        bias,
        block_weight,
    )
    nblocks = dp * shard // blk
    scale = 1.0 / math.sqrt(batch * dp)
    misfit, adj = pl.pallas_call(
        functools.partial(decode_kernel, scale),
        out_shape=(
            sds((tiles, batch, blk), BF16),
            sds((nblocks, blk, batch), BF16),
        ),
        in_specs=[smem, smem, vmem, vmem, vmem],
        out_specs=[vmem] * 2,
        scratch_shapes=[pltpu.VMEM((nblocks, blk, batch), F32)],
        compiler_params=pltpu.CompilerParams(vmem_limit_bytes=VMEM_LIMIT),
        name="decode",
    )(
        block_ids,
        block_counts,
        hid.reshape(nblocks, blk, batch),
        block_all.reshape(tiles, slots, blk, blk),
        snapshots,
    )
    weight_grad, bias_grad, enc_grad, mis_all = pl.pallas_call(
        functools.partial(backward_kernel, row, dp),
        out_shape=(
            sds((row, part, latent), BF16),
            sds((row, 8, part), F32),
            sds((cols, latent), F32),
            sds((dp, own, batch, blk), BF16),
        ),
        in_specs=[vmem] * 6,
        out_specs=[vmem] * 4,
        scratch_shapes=[
            pltpu.VMEM((dp, row // 2, part, batch), BF16),
            pltpu.VMEM((row // 2, dp, part, batch), BF16),
            pltpu.VMEM((row // 2, dp, part, batch), BF16),
            pltpu.VMEM((dp, part, batch), BF16),
            pltpu.VMEM((dp, part, batch), BF16),
            pltpu.VMEM((row, batch, latent), F32),
            pltpu.VMEM((dp, batch, latent), BF16),
            dma((3, dp)), dma((3, dp)), dma((3, row)), dma((3, row)), dma((2 * row,)), dma((row,)),
            dma((row // 2,)), dma((row // 2,)), dma((2,)),
        ],
        compiler_params=pltpu.CompilerParams(
            collective_id=1, has_side_effects=True, vmem_limit_bytes=VMEM_LIMIT
        ),
        name="backward",
    )(
        adj.reshape(dp, row // 2, 2, part, batch),
        misfit.reshape(dp, own, batch, blk),
        pre,
        lat_all,
        w_all,
        snap_all,
    )
    bias_lines = bias_all[:, :row].reshape(nblocks, 1, blk)
    block_grad = pl.pallas_call(
        block_grad_kernel,
        out_shape=sds((own, slots, blk, blk), F32),
        in_specs=[smem, smem, vmem, vmem, vmem, vmem],
        out_specs=vmem,
        compiler_params=pltpu.CompilerParams(vmem_limit_bytes=VMEM_LIMIT),
        name="block_grad",
    )(
        block_ids,
        block_counts,
        w_all.reshape(nblocks, blk, latent),
        jnp.pad(bias_lines, ((0, 0), (0, 15), (0, 0))),
        lat_all,
        mis_all,
    )
    return (
        enc_grad.reshape(own, blk, latent),
        weight_grad.reshape(shard, latent).astype(F32),
        bias_grad[:, 0, :].reshape(shard),
        block_grad,
    )


def solution(mesh):
    in_specs = (
        P(("groups", "dp"), "row"),
        P(("row", "dp"), None, None),
        P("dp", None),
        P("dp"),
        P(("row", "dp"), None, None, None),
        P("row", None),
        P("row"),
    )
    out_specs = (
        P(("groups", "row", "dp"), None, None),
        P(("groups", "dp"), None),
        P(("groups", "dp")),
        P(("groups", "row", "dp"), None, None, None),
    )
    return jax.shard_map(
        functools.partial(on_device, mesh.shape["groups"], mesh.shape["row"], mesh.shape["dp"]),
        mesh=mesh, in_specs=in_specs, out_specs=out_specs, check_vma=False,
    )
```
